256 devices in a mesh: segment: 8 (over y, x_hi), lon: 32 (over x_lo, z, core).
Axes of the slice: x: 4 (x_hi: 2, x_lo: 2; x = x_hi * 2 + x_lo), y: 4, z: 8, core: 2. Of those that a mesh axis runs over, the one named last changes fastest.
Arguments:
- fields: bfloat16 [4, 2, 12, 384, 192], P(None, None, None, 'lon'), may hold values from -6 to 6
- entry_order: int32 [4], replicated, may hold values from 0 to 3, each once
- shift_offsets: int32 [4, 2, 8], P(None, None, 'segment'), may hold values from 1 to 11
- qkv_weight: bfloat16 [2, 8, 192, 576], P(None, 'segment'), may hold values from -0.4375 to 0.4375
- out_weight: bfloat16 [2, 8, 192, 192], P(None, 'segment'), may hold values from -0.4375 to 0.4375
- up_weight: bfloat16 [2, 8, 192, 768], P(None, 'segment'), may hold values from -0.4375 to 0.4375
- down_weight: bfloat16 [2, 8, 768, 192], P(None, 'segment'), may hold values from -0.21875 to 0.21875
- attn_bias: float32 [2, 8, 2, 6, 144, 144], P(None, 'segment'), as said below
- norm_gain: float32 [2, 8, 2, 192], P(None, 'segment'), may hold values from 0.5 to 1.5
Outputs:
- result: bfloat16 [4, 2, 12, 384, 192], P(None, None, None, 'lon', 'segment')
The draws below stay inside these ranges and needn't reach their ends.
Inputs may be any that keep to these rules, and one draw needn't show every extreme that they name: `attn_bias`: entries are at least -6.
All inputs are finite; a program needn't handle non-finite values.
Results may differ from the reference program's by a relative error of at most 0.022.
Values may be sent and summed in bfloat16 or wider, within the bound.
A program may use at most 64 MiB of HBM per device.

```python
import jax
import jax.numpy as jnp
from jax import lax

C = 192
HEADS = 6
FF = 768
LEVELS = 2
WIN_LAT = 6
WIN_LON = 12
LAT = 12
MICRO = 4
SEGMENTS = 8
NLON = 384
LATW = 2
WT = 144


def draw_attn_bias(key, part):
    key = jax.random.fold_in(key, 11)
    keys = jax.random.split(key, 6)
    shape = (2, SEGMENTS, LATW, HEADS, WT, WT)
    rows = shape[:-1]
    base = jnp.clip(jax.random.normal(keys[0], shape, jnp.float32), -6.0, 6.0)
    chosen = jax.random.randint(keys[1], rows, 0, 50) == 0
    first = jax.random.randint(keys[2], rows, 0, WT)
    gap = jax.random.randint(keys[3], rows, 1, WT)
    second = (first + gap) % WT
    level = jax.random.randint(keys[4], rows, 0, 3)
    strength = jnp.where(level == 0, 120.0, jnp.where(level == 1, 200.0, 300.0))
    lowered = jax.random.uniform(keys[5], rows, jnp.float32, 1.0, 3.0)
    columns = jnp.arange(WT)
    hit_first = chosen[..., None] & (columns == first[..., None])
    hit_second = chosen[..., None] & (columns == second[..., None])
    result = jnp.where(hit_first, strength[..., None], jnp.where(hit_second, (strength - lowered)[..., None], base))
    return result.astype(jnp.float32)


def with_ends(values, rng, least, high):
    place = [jax.random.randint(jax.random.fold_in(rng, axis), (), 0, length) for axis, length in enumerate(values.shape)]
    widest = values.shape.index(max(values.shape))
    next_to = place[:widest] + [(place[widest] + 1) % values.shape[widest]] + place[widest + 1:]
    return values.at[tuple(place)].set(least).at[tuple(next_to)].set(high)


def block_scale(stream_key, shape, pieces, low, top_value):
    factor_of, own = 1.0, jax.random.fold_in(stream_key, 6)
    for dim, blocks in pieces:
        heights = jnp.exp(jax.random.uniform(jax.random.fold_in(own, dim), (blocks,), jnp.float32, low / len(pieces), top_value / len(pieces)))
        factor_of = factor_of * jnp.repeat(heights, shape[dim] // blocks).reshape([-1 if axis == dim else 1 for axis in range(len(shape))])
    return factor_of


def scatter_about(own_key, extent, scale, reach, shards=(), kind=jnp.bfloat16):
    array = jax.random.normal(own_key, extent, jnp.float32) * scale
    if len(shards) > 0:
        array = block_scale(own_key, extent, shards, -0.22, 0.18) * array
    return jnp.clip(array, min=-reach, max=reach).astype(kind)


def setup_inputs(seed: int = 0) -> dict:
    key_of = jax.random.split(jax.random.key(seed), 10)
    fields = scatter_about(key_of[0], (MICRO, LEVELS, LAT, NLON, C), 1.0, 6.0, ((3, 32),))
    entry_order = jax.random.permutation(key_of[1], MICRO).astype(jnp.int32)
    shift_offsets = with_ends(jax.random.randint(key_of[2], (MICRO, 2, SEGMENTS), 1, WIN_LON), jax.random.fold_in(key_of[2], 1), 1, WIN_LON - 1).astype(jnp.int32)
    qkv_weight = scatter_about(key_of[3], (2, SEGMENTS, C, 3 * C), C ** -0.5, 0.4375, ((1, 8),))
    out_weight = scatter_about(key_of[4], (2, SEGMENTS, C, C), C ** -0.5, 0.4375, ((1, 8),))
    up_weight = scatter_about(key_of[5], (2, SEGMENTS, C, FF), C ** -0.5, 0.4375, ((1, 8),))
    down_weight = scatter_about(key_of[6], (2, SEGMENTS, FF, C), FF ** -0.5, 0.21875, ((1, 8),))
    attn_bias = draw_attn_bias(jax.random.fold_in(key_of[9], 71), 0)
    norm_gain = jnp.clip(1.0 + 0.1 * jax.random.normal(key_of[8], (2, SEGMENTS, 2, C), jnp.float32), 0.5, 1.5)
    return dict(fields=fields, entry_order=entry_order, shift_offsets=shift_offsets, qkv_weight=qkv_weight, out_weight=out_weight, up_weight=up_weight, down_weight=down_weight, attn_bias=attn_bias, norm_gain=norm_gain)


EPS = 1e-05

def normalize(values, gain):
    average = lax.optimization_barrier(jnp.mean(values, axis=-1, keepdims=True))
    centred = values - average
    spread = lax.optimization_barrier(jnp.mean(centred * centred, axis=-1, keepdims=True))
    return centred * lax.rsqrt(spread + EPS) * gain

def to_windows(grid):
    levels, rows, cells, feats = grid.shape
    shaped = grid.reshape(levels, rows // WIN_LAT, WIN_LAT, cells // WIN_LON, WIN_LON, feats)
    shaped = shaped.transpose(1, 3, 0, 2, 4, 5)
    return shaped.reshape(rows // WIN_LAT, cells // WIN_LON, levels * WIN_LAT * WIN_LON, feats)

def from_windows(windows, levels):
    lat_count, lon_count, tokens, feats = windows.shape
    shaped = windows.reshape(lat_count, lon_count, levels, WIN_LAT, WIN_LON, feats)
    shaped = shaped.transpose(2, 0, 3, 1, 4, 5)
    return shaped.reshape(levels, lat_count * WIN_LAT, lon_count * WIN_LON, feats)

def section_block(source, gains, w_qkv, w_out, w_up, w_down, bias_table, offset):
    levels, rows, cells, width = source.shape
    head_dim = width // HEADS
    offset = offset.astype(jnp.int32)
    doubled = jnp.concatenate([source, source], axis=2)
    rolled = lax.dynamic_slice_in_dim(doubled, offset, cells, 2)
    normed_a = normalize(rolled.astype(jnp.float32), gains[0]).astype(jnp.bfloat16)
    packed = jnp.dot(normed_a.reshape(-1, width), w_qkv, preferred_element_type=jnp.float32)
    packed = packed.astype(jnp.bfloat16).reshape(levels, rows, cells, 3 * width)
    windows = to_windows(packed)
    lat_count, lon_count, tokens, _ = windows.shape
    queries = windows[..., :width].reshape(lat_count, lon_count, tokens, HEADS, head_dim)
    keys = windows[..., width:2 * width].reshape(lat_count, lon_count, tokens, HEADS, head_dim)
    values = windows[..., 2 * width:].reshape(lat_count, lon_count, tokens, HEADS, head_dim)
    scores = jnp.einsum('anqhd,ankhd->anhqk', queries.astype(jnp.float32), keys.astype(jnp.float32))
    scores = scores * head_dim ** (-0.5) + bias_table[:, None]
    highest = lax.optimization_barrier(jnp.max(scores, axis=-1, keepdims=True))
    expo = jnp.exp(scores - highest)
    probs = (expo / lax.optimization_barrier(jnp.sum(expo, axis=-1, keepdims=True))).astype(jnp.bfloat16)
    context = jnp.einsum('anhqk,ankhd->anqhd', probs.astype(jnp.float32), values.astype(jnp.float32))
    context = context.astype(jnp.bfloat16).reshape(lat_count, lon_count, tokens, width)
    grid = from_windows(context, levels)
    attended = jnp.dot(grid.reshape(-1, width), w_out, preferred_element_type=jnp.float32)
    attended = attended.astype(jnp.bfloat16).reshape(levels, rows, cells, width)
    doubled_out = jnp.concatenate([attended, attended], axis=2)
    restored = lax.dynamic_slice_in_dim(doubled_out, (cells - offset).astype(jnp.int32), cells, 2)
    first_sum = source.astype(jnp.float32) + restored.astype(jnp.float32)
    normed_b = normalize(first_sum, gains[1]).astype(jnp.bfloat16)
    hidden = jax.nn.gelu(jnp.dot(normed_b.reshape(-1, width), w_up, preferred_element_type=jnp.float32))
    hidden = hidden.astype(jnp.bfloat16)
    output = first_sum.reshape(-1, width) + jnp.dot(hidden, w_down, preferred_element_type=jnp.float32)
    return output.astype(jnp.bfloat16).reshape(levels, rows, cells, width)

def reference(fields, entry_order, shift_offsets, qkv_weight, out_weight, up_weight, down_weight, attn_bias, norm_gain):
    segments = qkv_weight.shape[1]

    def one_slot(slot):
        start = lax.dynamic_index_in_dim(fields, entry_order[slot], 0, keepdims=False)
        stored = jnp.zeros((segments,) + start.shape, jnp.bfloat16)

        def section(number, carried):
            current, stored = carried
            number = jnp.asarray(number).astype(jnp.int32)
            half = (number >= segments).astype(jnp.int32)
            index = jnp.where(number < segments, number, 2 * segments - 1 - number).astype(jnp.int32)
            skipped = lax.dynamic_index_in_dim(stored, index, 0, keepdims=False)
            merged = (0.5 * (current.astype(jnp.float32) + skipped.astype(jnp.float32))).astype(jnp.bfloat16)
            source = jnp.where(number > segments, merged, current)
            offset = shift_offsets[slot, half, index]
            output = section_block(source, norm_gain[half, index], qkv_weight[half, index], out_weight[half, index], up_weight[half, index], down_weight[half, index], attn_bias[half, index], offset)
            kept = jnp.where(number < segments, output, skipped)
            stored = lax.dynamic_update_index_in_dim(stored, kept, index, 0)
            return (output, stored)
        final, _ = lax.fori_loop(0, 2 * segments, section, (start, stored))
        return final
    outputs = lax.map(one_slot, jnp.arange(MICRO, dtype=jnp.int32))
    return jnp.zeros_like(outputs).at[entry_order].set(outputs)
```

```python
import functools
import math

import jax
import jax.numpy as jnp
from jax import lax
from jax.experimental import pallas as pl
from jax.experimental.pallas import tpu as pltpu
from jax.sharding import PartitionSpec as P

BF = jnp.bfloat16
F32 = jnp.float32
MESH = pl.DeviceIdType.MESH
NT = (((1,), (1,)), ((), ()))
TN = (((0,), (0,)), ((), ()))
NN = (((1,), (0,)), ((), ()))

SEGS = 8
SECTIONS = 16
HEADS = 6
TOK = 144
WIDTH = 192
LON = 12
STRIP = 192
HALF_W = 9 * STRIP
HALF_B = 4 * TOK
HALF = HALF_W + HALF_B
PACK = 2 * HALF
PARAMS = HALF + HALF_W + 3 * TOK
EPS = 1e-5
QSCALE = math.log2(math.e) / math.sqrt(32.0)


def dot(a, b, dims=NN):
    return lax.dot_general(a, b, dims, preferred_element_type=F32)


def side(parts):
    return jnp.concatenate(parts, axis=1)


def down(parts):
    return jnp.concatenate(parts, axis=0)


def lanes(shape):
    return lax.broadcasted_iota(jnp.int32, shape, len(shape) - 1)


def normalize(x, gain, inside):
    mean = jnp.sum(x, axis=-1, keepdims=True) * (1.0 / WIDTH)
    centred = x - mean * inside
    spread = jnp.sum(centred * centred, axis=-1, keepdims=True) * (1.0 / WIDTH)
    return (centred * lax.rsqrt(spread + EPS) * gain).astype(BF)


def pick(lon, shift):
    row = lax.broadcasted_iota(jnp.int32, (TOK, 128), 0).astype(F32)
    x = lon + shift
    wrap = jnp.where(x < 0, float(LON - TOK), jnp.where(x > LON - 1, float(TOK - LON), 0.0))
    target = row + shift + wrap + float(TOK)
    col = lanes((TOK, 128)).astype(F32)
    tiles = [jnp.where(col + float(128 * j) == target, 1.0, 0.0).astype(BF) for j in range(4)]
    return side(tiles)[:, : 3 * TOK]


def section(u, strip, bias, gain_a, gain_b):
    col = lanes((1, 256))
    inside = jnp.where(col < WIDTH, 1.0, 0.0)
    low = jnp.where(lanes((1, 128)) < 64, 1.0, 0.0)
    normed = normalize(u, gain_a, inside)
    short = normed[:, :WIDTH]
    qk = dot(short, side([strip(0), strip(1), strip(2)]))
    qb = (qk[:, :256] * QSCALE).astype(BF)
    kb = side([qk[:, 256:], pltpu.roll(qk[:, 128:256], 64, 1)]).astype(BF)
    mixed = strip(4)
    vt = dot(side([strip(3), mixed]), normed, NT).astype(BF)
    zero = jnp.zeros((TOK, 256), BF)
    pos = lanes((TOK, 256))
    spread_q = down(
        [jnp.where((pos >= 32 * h) & (pos < 32 * h + 32), qb, zero) for h in range(HEADS)]
        + [jnp.zeros((32, 256), BF)]
    )
    scores = dot(kb, spread_q, NT) + side([bias(j) for j in range(7)]).astype(F32)
    top = jnp.max(scores, axis=0, keepdims=True)
    expo = jnp.exp2(scores - top)
    inverse = 1.0 / jnp.sum(expo, axis=0, keepdims=True)
    expo = expo.astype(BF)
    parts = []
    for h in range(HEADS):
        cut = slice(128 * h, 128 * h + 256)
        part = dot(vt[32 * h : 32 * h + 32], expo[:, cut]) * inverse[:, cut]
        if h:
            part = pltpu.roll(part, 256 - 16 * h, 1)
        parts.append(part[:, :TOK])
    context = down(parts).astype(BF)
    out = dot(context, side([strip(5), mixed]), TN)
    out = side([out[:, :128], pltpu.roll(out[:, 128:], 64, 1) * low])
    x1 = u + out.astype(BF).astype(F32)
    normed = normalize(x1, gain_b, inside)[:, :WIDTH]
    hidden = jax.nn.gelu(dot(normed, side([strip(6 + j) for j in range(6)]))).astype(BF)
    tail = down([strip(16), strip(17)])
    y0 = dot(hidden[:, :384], side([down([strip(12), strip(13)]), tail]))
    y1 = dot(hidden[:, 384:], side([down([strip(14), strip(15)]), tail]))
    y = side([y0[:, :128] + y1[:, :128], (y0[:, 128:] + pltpu.roll(y1[:, 128:], 64, 1)) * low])
    return (x1 + y).astype(BF)


def kernel(
    x_ref, own_ref, other_ref, out_ref,
    packs, hist, lon_ref, pieces, received,
    local_sem, w_send, w_recv, s_send, s_recv, h_send, h_recv, f_send, f_recv,
):
    seg = lax.axis_index("segment")
    me = lax.axis_index("lon")
    ring = lax.axis_size("lon")
    core = lax.rem(me, 2)
    sibling = me + 1 - 2 * core
    west = lax.rem(me + ring - 1, ring)
    east = lax.rem(me + 1, ring)
    slot = seg // 2
    lat = lax.rem(seg, 2)

    fills = [
        pltpu.make_async_copy(
            own_ref.at[half], packs.at[seg if half == 0 else 15 - seg], local_sem.at[half]
        )
        for half in range(2)
    ]
    for fill in fills:
        fill.start()

    barrier = pltpu.get_barrier_semaphore()
    for d in range(1, SEGS):
        pl.semaphore_signal(
            barrier, inc=1, device_id=(lax.rem(seg + d, SEGS), me), device_id_type=MESH
        )
    for lon_to in (west, east):
        pl.semaphore_signal(barrier, inc=1, device_id=(seg, lon_to), device_id_type=MESH)
    pl.semaphore_wait(barrier, SEGS + 1)

    def source(number):
        return jnp.minimum(number, SECTIONS - 1 - number)

    def weight_copy(half, d, number):
        there = lax.rem(seg + d, SEGS)
        start = pl.multiple_of(core * HALF, 16)
        return pltpu.make_async_remote_copy(
            packs.at[number, pl.ds(start, HALF)],
            packs.at[number, pl.ds(start, HALF)],
            w_send.at[half, d],
            w_recv.at[number],
            device_id=(there, me),
            device_id_type=MESH,
        )

    def send_weights(half):
        number = seg if half == 0 else 15 - seg
        start = pl.multiple_of(core * HALF, 16)
        b_start = pl.multiple_of(core * HALF + HALF_W, 16)
        for d in (1, 7, 2, 6, 3, 5, 4):
            there = lax.rem(seg + d, SEGS)
            if d % 2 == 0:
                weight_copy(half, d, number).start()
            else:
                pltpu.make_async_remote_copy(
                    packs.at[number, pl.ds(start, HALF_W)],
                    packs.at[number, pl.ds(start, HALF_W)],
                    w_send.at[half, d],
                    w_recv.at[number],
                    device_id=(there, me),
                    device_id_type=MESH,
                ).start()
                pltpu.make_async_remote_copy(
                    other_ref.at[half, core],
                    packs.at[number, pl.ds(b_start, HALF_B)],
                    w_send.at[half, d],
                    w_recv.at[number],
                    device_id=(there, me),
                    device_id_type=MESH,
                ).start()

    def relay_copy(number):
        start = pl.multiple_of(core * HALF, 16)
        return pltpu.make_async_remote_copy(
            packs.at[number, pl.ds(start, HALF)],
            packs.at[number, pl.ds(start, HALF)],
            s_send.at[number],
            s_recv.at[number],
            device_id=(seg, sibling),
            device_id_type=MESH,
        )

    def relay_wait(number):
        start = pl.multiple_of((1 - core) * HALF, 16)
        pltpu.make_async_remote_copy(
            packs.at[number, pl.ds(start, HALF)],
            packs.at[number, pl.ds(start, HALF)],
            s_send.at[number],
            s_recv.at[number],
            device_id=(seg, sibling),
            device_id_type=MESH,
        ).wait_recv()

    def relay(number):
        @pl.when(source(number) != seg)
        def _():
            weight_copy(0, 1, number).wait_recv()
            relay_copy(number).start()

    def halo_copy(number, way):
        return pltpu.make_async_remote_copy(
            hist.at[number, pl.ds(TOK, TOK)],
            hist.at[number, pl.ds(2 * TOK if way == 0 else 0, TOK)],
            h_send.at[number, way],
            h_recv.at[number, way],
            device_id=(seg, west if way == 0 else east),
            device_id_type=MESH,
        )

    hist[0, TOK : 2 * TOK] = x_ref[...]
    for way in range(2):
        halo_copy(0, way).start()
    for fill in fills:
        fill.wait()
    send_weights(0)
    token = lax.broadcasted_iota(jnp.int32, (TOK, 128), 0)
    lon_ref[...] = lax.rem(token, LON).astype(F32)
    relay(0)

    def params(number):
        return packs[number, PARAMS : PARAMS + 16, :].astype(F32)

    def offset(tile):
        row = lax.broadcasted_iota(jnp.int32, (16, 128), 0)
        return jnp.sum(jnp.where(row == 12 + slot, tile, 0.0), axis=0, keepdims=True)

    def step(number, decoder):
        if not decoder:
            @pl.when(number == 0)
            def _():
                send_weights(1)

        @pl.when(number < SECTIONS - 1)
        def _():
            relay(number + 1)

        @pl.when(source(number) != seg)
        def _():
            relay_wait(number)

        tile = params(number)
        now = offset(tile)
        if decoder:
            before = offset(params(number - 1))
            aside = dot(pick(lon_ref[...], now - offset(params(15 - number))), hist[16 - number])
        else:
            before = offset(params(jnp.maximum(number - 1, 0)))
            before = before * jnp.where(number > 0, 1.0, 0.0)
        chosen = pick(lon_ref[...], now - before)
        for way in range(2):
            halo_copy(number, way).wait_recv()
        u = dot(chosen, hist[number])
        if decoder:
            u = ((u + aside) * 0.5).astype(BF).astype(F32)
        gain_a = side([tile[0:1] + tile[2:3] + tile[4:5], tile[1:2] + tile[3:4] + tile[5:6]])
        gain_b = side([tile[6:7] + tile[8:9] + tile[10:11], tile[7:8] + tile[9:10] + tile[11:12]])

        def strip(j):
            start = STRIP * j if j < 9 else HALF + STRIP * (j - 9)
            return packs[number, start : start + STRIP, :]

        def bias(j):
            start = HALF_W + TOK * j if j < 4 else HALF + HALF_W + TOK * (j - 4)
            return packs[number, start : start + TOK, :]

        hist[number + 1, TOK : 2 * TOK] = section(u, strip, bias, gain_a, gain_b)
        for way in range(2):
            halo_copy(number + 1, way).start()

    lax.fori_loop(0, 9, lambda i, c: (step(i, False), c)[1], 0)
    lax.fori_loop(9, SECTIONS, lambda i, c: (step(i, True), c)[1], 0)

    back = pick(lon_ref[...], -offset(params(SECTIONS - 1)))
    for way in range(2):
        halo_copy(SECTIONS, way).wait_recv()
    final = dot(back, hist[SECTIONS])
    share = WIDTH // SEGS
    for s in range(SEGS):
        pieces[s, :, :share] = final[:, share * s : share * (s + 1)].astype(BF)

    def piece_copy(d):
        there = lax.rem(seg + d, SEGS)
        return pltpu.make_async_remote_copy(
            pieces.at[there],
            received.at[seg],
            f_send.at[d],
            f_recv.at[d],
            device_id=(there, me),
            device_id_type=MESH,
        )

    for d in range(1, SEGS):
        piece_copy(d).start()
    mine = pltpu.make_async_copy(pieces.at[seg], received.at[seg], local_sem.at[0])
    mine.start()

    for half in range(2):
        number = seg if half == 0 else 15 - seg
        for d in range(1, SEGS):
            weight_copy(half, d, number).wait_send()
    for number in range(SECTIONS):
        @pl.when(source(number) != seg)
        def _():
            relay_copy(number).wait_send()
    for number in range(SECTIONS + 1):
        for way in range(2):
            halo_copy(number, way).wait_send()
    mine.wait()
    for d in range(1, SEGS):
        piece_copy(d).wait()
    out_ref[...] = received[...]


def split3(x):
    high = x.astype(BF)
    rest = x - high.astype(F32)
    middle = rest.astype(BF)
    return high, middle, (rest - middle.astype(F32)).astype(BF)


def pack_weights(qkv, out, up, low, gains, shifts, bias, lat):
    q, k, v = qkv[:, :192], qkv[:, 192:384], qkv[:, 384:].T
    strips = [
        q[:, :128], side([q[:, 128:], k[:, 128:]]), k[:, :128],
        v[:, :128], side([v[:, 128:], out[:, 128:]]), out[:, :128],
    ]
    strips += [up[:, 128 * j : 128 * j + 128] for j in range(6)]
    strips += [low[:, :128], side([low[:384, 128:], low[384:, 128:]])]
    weights = down(strips).reshape(2, HALF_W, 128)
    top = jnp.max(bias, axis=-1, keepdims=True)
    bias = ((bias - top) * math.log2(math.e)).astype(BF)
    bias = bias.transpose(0, 3, 1, 2).reshape(2, TOK, HEADS * TOK)
    bias = jnp.pad(bias, ((0, 0), (0, 0), (0, 1024 - HEADS * TOK)))
    bias = bias.reshape(2, TOK, 8, 128).transpose(0, 2, 1, 3)
    rows = []
    for gain in gains:
        for part in split3(gain):
            rows += [part[:128], jnp.pad(part[128:], (0, 64))]
    rows += [jnp.full((128,), shifts[t]).astype(BF) for t in range(4)]
    small = jnp.stack(rows)
    bias = bias.reshape(2, 8 * TOK, 128)
    bias = jnp.concatenate(
        [bias[:, : 7 * TOK], jnp.broadcast_to(small, (2, 16, 128)), bias[:, 7 * TOK + 16 :]], axis=1
    ).reshape(2, 2, HALF_B, 128)
    here = lax.dynamic_index_in_dim(bias, lat, 0, keepdims=False)
    there = lax.dynamic_index_in_dim(bias, 1 - lat, 0, keepdims=False)
    own = jnp.concatenate([weights, here], axis=1).reshape(PACK, 128)
    return own, there


def per_device(
    fields, entry_order, shift_offsets, qkv_weight, out_weight, up_weight, down_weight,
    attn_bias, norm_gain,
):
    seg = lax.axis_index("segment")
    slot, lat = seg // 2, lax.rem(seg, 2)
    grid = lax.dynamic_slice(
        fields, (entry_order[slot], 0, 6 * lat, 0, 0), (1, 2, 6, LON, WIDTH)
    )
    x = jnp.pad(grid.reshape(TOK, WIDTH), ((0, 0), (0, 64)))
    packed = [
        pack_weights(
            qkv_weight[h, 0], out_weight[h, 0], up_weight[h, 0], down_weight[h, 0],
            norm_gain[h, 0], shift_offsets[:, h, 0], attn_bias[h, 0], lat,
        )
        for h in range(2)
    ]
    own = jnp.stack([p[0] for p in packed])
    other = jnp.stack([p[1] for p in packed])
    dma = pltpu.SemaphoreType.DMA
    got = pl.pallas_call(
        kernel,
        out_shape=jax.ShapeDtypeStruct((SEGS, TOK, 128), BF),
        in_specs=[pl.BlockSpec(memory_space=pltpu.VMEM), pl.BlockSpec(memory_space=pl.ANY),
                  pl.BlockSpec(memory_space=pl.ANY)],
        out_specs=pl.BlockSpec(memory_space=pltpu.VMEM),
        scratch_shapes=[
            pltpu.VMEM((SECTIONS, PACK, 128), BF),
            pltpu.VMEM((SECTIONS + 1, 3 * TOK, 256), BF),
            pltpu.VMEM((TOK, 128), F32),
            pltpu.VMEM((SEGS, TOK, 128), BF),
            pltpu.VMEM((SEGS, TOK, 128), BF),
            dma((2,)), dma((2, SEGS)), dma((SECTIONS,)), dma((SECTIONS,)), dma((SECTIONS,)),
            dma((SECTIONS + 1, 2)), dma((SECTIONS + 1, 2)), dma((SEGS,)), dma((SEGS,)),
        ],
        compiler_params=pltpu.CompilerParams(
            collective_id=0, has_side_effects=True, vmem_limit_bytes=50 * 2**20
        ),
        name="sections",
    )(x, own, other)
    share = WIDTH // SEGS
    got = got[:, :, :share].reshape(4, 2, 2, 6, LON, share).transpose(0, 2, 1, 3, 4, 5)
    got = got.reshape(4, 2, 12, LON, share)
    chosen = (entry_order[None, :] == jnp.arange(4)[:, None]).astype(jnp.int32)
    place = jnp.sum(chosen * jnp.arange(4)[None, :], axis=1)
    return jnp.take(got, place, axis=0)


def solution(mesh):
    placed = (
        P(None, None, None, "lon", None),
        P(),
        P(None, None, "segment"),
        P(None, "segment", None, None),
        P(None, "segment", None, None),
        P(None, "segment", None, None),
        P(None, "segment", None, None),
        P(None, "segment", None, None, None, None),
        P(None, "segment", None, None),
    )
    return jax.shard_map(
        per_device,
        mesh=mesh,
        in_specs=placed,
        out_specs=P(None, None, None, "lon", "segment"),
        check_vma=False,
    )
```

```python
import functools
import math

import jax
import jax.numpy as jnp
from jax import lax
from jax.experimental import pallas as pl
from jax.experimental.pallas import tpu as pltpu
from jax.sharding import PartitionSpec as P

BF = jnp.bfloat16
F32 = jnp.float32
MESH = pl.DeviceIdType.MESH
NT = (((1,), (1,)), ((), ()))
TN = (((0,), (0,)), ((), ()))
NN = (((1,), (0,)), ((), ()))

SEGS = 8
SECTIONS = 16
EARLY = 3
HEADS = 6
TOK = 144
WIDTH = 192
LON = 12
STRIP = 192
HALF_W = 9 * STRIP
HALF_B = 4 * TOK
HALF = HALF_W + HALF_B
PACK = 2 * HALF
PARAMS = HALF + HALF_W + 3 * TOK
EPS = 1e-5
QSCALE = math.log2(math.e) / math.sqrt(32.0)


def dot(a, b, dims=NN):
    return lax.dot_general(a, b, dims, preferred_element_type=F32)


def side(parts):
    return jnp.concatenate(parts, axis=1)


def down(parts):
    return jnp.concatenate(parts, axis=0)


def lanes(shape):
    return lax.broadcasted_iota(jnp.int32, shape, len(shape) - 1)


def normalize(x, gain, inside):
    mean = jnp.sum(x, axis=-1, keepdims=True) * (1.0 / WIDTH)
    centred = x - mean * inside
    spread = jnp.sum(centred * centred, axis=-1, keepdims=True) * (1.0 / WIDTH)
    return (centred * lax.rsqrt(spread + EPS) * gain).astype(BF)


def pick(lon, shift):
    row = lax.broadcasted_iota(jnp.int32, (TOK, 128), 0).astype(F32)
    x = lon + shift
    wrap = jnp.where(x < 0, float(LON - TOK), jnp.where(x > LON - 1, float(TOK - LON), 0.0))
    target = row + shift + wrap + float(TOK)
    col = lanes((TOK, 128)).astype(F32)
    tiles = [jnp.where(col + float(128 * j) == target, 1.0, 0.0).astype(BF) for j in range(4)]
    return side(tiles)[:, : 3 * TOK]


def section(u, strip, bias, gain_a, gain_b):
    col = lanes((1, 256))
    inside = jnp.where(col < WIDTH, 1.0, 0.0)
    low = jnp.where(lanes((1, 128)) < 64, 1.0, 0.0)
    normed = normalize(u, gain_a, inside)
    short = normed[:, :WIDTH]
    qk = dot(short, side([strip(0), strip(1), strip(2)]))
    qb = (qk[:, :256] * QSCALE).astype(BF)
    kb = side([qk[:, 256:], pltpu.roll(qk[:, 128:256], 64, 1)]).astype(BF)
    mixed = strip(4)
    vt = dot(side([strip(3), mixed]), normed, NT).astype(BF)
    zero = jnp.zeros((TOK, 256), BF)
    pos = lanes((TOK, 256))
    spread_q = down(
        [jnp.where((pos >= 32 * h) & (pos < 32 * h + 32), qb, zero) for h in range(HEADS)]
        + [jnp.zeros((32, 256), BF)]
    )
    scores = dot(kb, spread_q, NT) + side([bias(j) for j in range(7)]).astype(F32)
    top = jnp.max(scores, axis=0, keepdims=True)
    expo = jnp.exp2(scores - top)
    inverse = 1.0 / jnp.sum(expo, axis=0, keepdims=True)
    expo = expo.astype(BF)
    parts = []
    for h in range(HEADS):
        cut = slice(128 * h, 128 * h + 256)
        part = dot(vt[32 * h : 32 * h + 32], expo[:, cut]) * inverse[:, cut]
        if h:
            part = pltpu.roll(part, 256 - 16 * h, 1)
        parts.append(part[:, :TOK])
    context = down(parts).astype(BF)
    out = dot(context, side([strip(5), mixed]), TN)
    out = side([out[:, :128], pltpu.roll(out[:, 128:], 64, 1) * low])
    x1 = u + out.astype(BF).astype(F32)
    normed = normalize(x1, gain_b, inside)[:, :WIDTH]
    hidden = jax.nn.gelu(dot(normed, side([strip(6 + j) for j in range(6)]))).astype(BF)
    tail = down([strip(16), strip(17)])
    y0 = dot(hidden[:, :384], side([down([strip(12), strip(13)]), tail]))
    y1 = dot(hidden[:, 384:], side([down([strip(14), strip(15)]), tail]))
    y = side([y0[:, :128] + y1[:, :128], (y0[:, 128:] + pltpu.roll(y1[:, 128:], 64, 1)) * low])
    return (x1 + y).astype(BF)


def kernel(
    fields_ref, order_ref, shift_ref, qkv_ref, out_w_ref, up_ref, low_ref, bias_ref, gain_ref,
    out_ref,
    packs, other, hist, lon_ref, stage, swap, gains, pieces, received,
    local_sem, swap_sem, a_send, a_recv, b_send, b_recv, x_send, x_recv,
    c_send, c_recv, w_send, w_recv, s_send, s_recv, h_send, h_recv, f_send, f_recv,
):
    seg = lax.axis_index("segment")
    me = lax.axis_index("lon")
    ring = lax.axis_size("lon")
    half_ring = ring // 2
    core = lax.rem(me, 2)
    sibling = me + 1 - 2 * core
    column = lax.rem(seg, 2)
    facing = seg + 1 - 2 * column
    slot = column + 2 * (seg // 4)
    lat = lax.rem(seg // 2, 2)
    across = lax.rem(me + half_ring, ring)
    folded = me >= half_ring

    def along(place):
        place = lax.rem(place + ring, ring)
        return jnp.where(place < half_ring, place, 3 * half_ring - 1 - place)

    place = along(me)
    west, east = along(place - 1), along(place + 1)

    barrier = pltpu.get_barrier_semaphore()

    def greet(seg_to, lon_to):
        pl.semaphore_signal(barrier, inc=1, device_id=(seg_to, lon_to), device_id_type=MESH)

    for d in (2, 4, 6):
        greet(lax.rem(seg + d, SEGS), me)
    greet(facing, across)
    greet(seg, west)
    greet(seg, east)
    for d in range(1, SEGS):
        greet(lax.rem(seg + d, SEGS), place)
    greet(seg, jnp.where(folded, place, sibling))
    chips = half_ring // 2
    chip = lax.rem(me, half_ring) // 2
    plane = me // half_ring

    def on_chip(n):
        return plane * half_ring + 2 * lax.rem(chip + n, chips) + core

    for n in range(1, chips):
        greet(seg, on_chip(n))
    greet(seg, across)
    for n in range(1, 4):
        greet(lax.rem(facing + 2 * n, SEGS), across)

    def source(number):
        return jnp.minimum(number, SECTIONS - 1 - number)

    def own_number(half):
        return seg if half == 0 else SECTIONS - 1 - seg

    def prepare(half):
        number = own_number(half)

        def put(start, block):
            block = block.astype(BF)
            packs[number, start : start + block.shape[0], :] = block
            other[half, start : start + block.shape[0], :] = block

        def put_strip(j, block):
            put(STRIP * j if j < 9 else HALF + STRIP * (j - 9), block)

        low = lanes((STRIP, 128)) < 64
        qkv = [qkv_ref[half, :, 128 * j : 128 * j + 128].astype(F32) for j in range(4)]
        put_strip(0, qkv[0])
        put_strip(1, jnp.where(low, qkv[1], qkv[2]))
        put_strip(2, jnp.where(low, pltpu.roll(qkv[1], 64, 1), pltpu.roll(qkv[2], 64, 1)))
        eye = (lax.broadcasted_iota(jnp.int32, (WIDTH, WIDTH), 0) == lanes((WIDTH, WIDTH)))
        turned = dot(jnp.where(eye, 1.0, 0.0).astype(BF), qkv_ref[half, :, 384:576], NT)
        out_w = out_w_ref[half].astype(F32)
        put_strip(3, turned[:, :128])
        put_strip(4, side([turned[:, 128:], out_w[:, 128:]]))
        put_strip(5, out_w[:, :128])
        for j in range(6):
            put_strip(6 + j, up_ref[half, :, 128 * j : 128 * j + 128])
        for j in range(4):
            put_strip(12 + j, low_ref[half, STRIP * j : STRIP * j + STRIP, :128])
        for j in range(2):
            upper = low_ref[half, STRIP * j : STRIP * j + STRIP, 128:].astype(F32)
            lower = low_ref[half, 384 + STRIP * j : 384 + STRIP * j + STRIP, 128:].astype(F32)
            put_strip(16 + j, side([upper, lower]))

        eye = (lax.broadcasted_iota(jnp.int32, (TOK, TOK), 0) == lanes((TOK, TOK)))
        eye = jnp.where(eye, 1.0, 0.0).astype(BF)

        def put_bias(window, store):
            table = bias_ref[half, window].reshape(HEADS * TOK, TOK)
            top = jnp.max(table, axis=-1, keepdims=True)
            table = ((table - top) * math.log2(math.e)).astype(BF)
            table = dot(eye, down([table, jnp.zeros((32, TOK), BF)]), NT).astype(BF)
            for j in range(7):
                start = HALF_W + TOK * j if j < 4 else HALF + HALF_W + TOK * (j - 4)
                store(start, table[:, 128 * j : 128 * j + 128])

        def store_own(start, block):
            packs[number, start : start + TOK, :] = block

        def store_other(start, block):
            other[half, start : start + TOK, :] = block

        put_bias(lat, store_own)
        put_bias(1 - lat, store_other)
        gains[...] = jnp.zeros_like(gains)
        gains[0:2, :WIDTH] = gain_ref[half]
        rows = []
        for n in range(2):
            for part in split3(gains[n : n + 1, :]):
                rows += [part[:, :128], part[:, 128:]]
        rows += [jnp.full((1, 128), shift_ref[t, half].astype(F32)) for t in range(4)]
        put(PARAMS, down(rows))
        rest = jnp.zeros((TOK - 16, 128), BF)
        put(PARAMS + 16, rest)

    half_rows = pl.ds(pl.multiple_of(core * HALF, 16), HALF)

    def part_rows(plane_of):
        start = core * HALF + plane_of * (HALF // 2)
        return pl.ds(pl.multiple_of(start, 16), HALF // 2)

    def own_copy(half, n):
        number = own_number(half)
        ref = packs.at[number] if n == 2 else other.at[half]
        return pltpu.make_async_remote_copy(
            ref.at[half_rows], packs.at[number, half_rows], w_send.at[half, n], w_recv.at[number],
            device_id=(lax.rem(seg + 2 * n, SEGS), me), device_id_type=MESH,
        )

    def send_weights(half):
        facing_copy(own_number(half)).start()
        for n in (1, 3, 2):
            own_copy(half, n).start()

    def facing_copy(number):
        rows = part_rows(plane)
        return pltpu.make_async_remote_copy(
            packs.at[number, rows], packs.at[number, rows], c_send.at[number], c_recv.at[number],
            device_id=(facing, across), device_id_type=MESH,
        )

    def cross_copy(number, plane_of):
        rows = part_rows(plane_of)
        return pltpu.make_async_remote_copy(
            packs.at[number, rows], packs.at[number, rows], x_send.at[number], x_recv.at[number],
            device_id=(seg, across), device_id_type=MESH,
        )

    def sibling_copy(number, start):
        start = pl.multiple_of(start * HALF, 16)
        return pltpu.make_async_remote_copy(
            packs.at[number, pl.ds(start, HALF)],
            packs.at[number, pl.ds(start, HALF)],
            s_send.at[number],
            s_recv.at[number],
            device_id=(seg, sibling),
            device_id_type=MESH,
        )

    def first(number):
        seg_of = source(number)

        @pl.when((seg_of != seg) & (lax.rem(seg_of, 2) == column))
        def _():
            pltpu.make_async_remote_copy(
                packs.at[number, half_rows], packs.at[number, half_rows], w_send.at[0, 0],
                w_recv.at[number], device_id=(facing, across), device_id_type=MESH,
            ).wait_recv()
            facing_copy(number).start()
            sibling_copy(number, core).start()

    def second(number):
        @pl.when(lax.rem(source(number), 2) != column)
        def _():
            rows = part_rows(1 - plane)
            pltpu.make_async_remote_copy(
                packs.at[number, rows], packs.at[number, rows], c_send.at[number],
                c_recv.at[number], device_id=(facing, across), device_id_type=MESH,
            ).wait_recv()
            cross_copy(number, 1 - plane).start()

    def third(number):
        @pl.when(lax.rem(source(number), 2) != column)
        def _():
            cross_copy(number, plane).wait_recv()
            sibling_copy(number, core).start()

    cut = HALF // 2 // chips

    def cut_rows(plane_of, chip_of):
        start = core * HALF + plane_of * (HALF // 2) + chip_of * cut
        return pl.ds(pl.multiple_of(start, 16), cut)

    def cut_copy(n):
        if n < 4:
            seg_to, lon_to, rows = seg + 2 * n, me, cut_rows(plane, chip)
        else:
            seg_to, lon_to, rows = facing + 2 * n, across, cut_rows(1 - plane, chip)
        ref = other.at[0] if n % 2 else packs.at[seg]
        return pltpu.make_async_remote_copy(
            ref.at[rows], packs.at[seg, rows], a_send.at[n], a_recv.at[jnp.minimum(seg, EARLY - 1)],
            device_id=(lax.rem(seg_to, SEGS), lon_to), device_id_type=MESH,
        )

    def send_cuts():
        for n in (4, 1, 3, 5, 7, 2, 6):
            cut_copy(n).start()

    def spread_copy(number, n):
        rows = cut_rows(plane, chip)
        return pltpu.make_async_remote_copy(
            packs.at[number, rows], packs.at[number, rows], b_send.at[number, n], b_recv.at[number],
            device_id=(seg, on_chip(n)), device_id_type=MESH,
        )

    def spread(number):
        @pl.when(seg != number)
        def _():
            rows = cut_rows(plane, chip)
            pltpu.make_async_remote_copy(
                packs.at[number, rows], packs.at[number, rows], a_send.at[0], a_recv.at[number],
                device_id=(seg, across), device_id_type=MESH,
            ).wait_recv()
            for n in (1, chips - 1, 2, chips - 2, 3, chips - 3, 4):
                if 0 < n < chips:
                    spread_copy(number, n).start()

    def cross(number):
        @pl.when(seg != number)
        def _():
            start = core * HALF + plane * (HALF // 2)
            rows = pl.ds(pl.multiple_of(start, 16), HALF // 2 - cut)
            if chips > 1:
                pltpu.make_async_remote_copy(
                    packs.at[number, rows], packs.at[number, rows], b_send.at[number, 0],
                    b_recv.at[number], device_id=(seg, across), device_id_type=MESH,
                ).wait_recv()
            cross_copy(number, plane).start()

    def pair_up(number):
        @pl.when(seg != number)
        def _():
            cross_copy(number, 1 - plane).wait_recv()
            sibling_copy(number, core).start()

    def halo_copy(number, way):
        return pltpu.make_async_remote_copy(
            hist.at[number, pl.ds(TOK, TOK)],
            hist.at[number, pl.ds(2 * TOK if way == 0 else 0, TOK)],
            h_send.at[number, way],
            h_recv.at[number, way],
            device_id=(seg, west if way == 0 else east),
            device_id_type=MESH,
        )

    swap_copy = pltpu.make_async_remote_copy(
        swap, hist.at[0, pl.ds(TOK, TOK)], swap_sem.at[0], swap_sem.at[1],
        device_id=(seg, place), device_id_type=MESH,
    )

    prepare(0)
    stage[...] = jnp.zeros_like(stage)
    micro = order_ref[slot]
    for n in range(12):
        stage[12 * n : 12 * n + 12, :WIDTH] = fields_ref[micro, n // 6, lat, n % 6].astype(F32)

    pl.semaphore_wait(barrier, 14 + chips + 3)

    @pl.when(seg < EARLY)
    def _():
        send_cuts()

    @pl.when(seg >= EARLY)
    def _():
        send_weights(0)


    @pl.when(folded)
    def _():
        swap[...] = stage[...].astype(BF)
        swap_copy.start()
        swap_copy.wait_recv()

    @pl.when(jnp.logical_not(folded))
    def _():
        hist[0, TOK : 2 * TOK] = stage[...].astype(BF)

    for way in range(2):
        halo_copy(0, way).start()
    token = lax.broadcasted_iota(jnp.int32, (TOK, 128), 0)
    lon_ref[...] = lax.rem(token, LON).astype(F32)
    spread(0)
    prepare(1)
    cross(0)
    spread(1)
    pair_up(0)

    def params(number):
        return packs[number, PARAMS : PARAMS + 16, :].astype(F32)

    def offset(tile):
        row = lax.broadcasted_iota(jnp.int32, (16, 128), 0)
        return jnp.sum(jnp.where(row == 12 + slot, tile, 0.0), axis=0, keepdims=True)

    def step(number, decoder):
        if not decoder:
            @pl.when(number == 0)
            def _():
                @pl.when(seg >= SEGS // 2)
                def _():
                    send_weights(1)

                cross(1)
                spread(2)

            @pl.when(number == 1)
            def _():
                pair_up(1)
                for n in range(EARLY, 7):
                    first(n)
                cross(2)

            @pl.when(number == 2)
            def _():
                @pl.when(seg < SEGS // 2)
                def _():
                    send_weights(1)

                pair_up(2)
                for n in range(EARLY, 6):
                    second(n)

            @pl.when(number == 3)
            def _():
                third(3)
                third(4)

        @pl.when((number >= 2) & (number < SECTIONS - 5))
        def _():
            first(number + 5)

        @pl.when((number >= 3) & (number < SECTIONS - 3))
        def _():
            second(number + 3)

        @pl.when((number >= 4) & (number < SECTIONS - 1))
        def _():
            third(number + 1)

        @pl.when(source(number) != seg)
        def _():
            sibling_copy(number, 1 - core).wait_recv()

        tile = params(number)
        now = offset(tile)
        if decoder:
            before = offset(params(number - 1))
            aside = dot(pick(lon_ref[...], now - offset(params(15 - number))), hist[16 - number])
        else:
            before = offset(params(jnp.maximum(number - 1, 0)))
            before = before * jnp.where(number > 0, 1.0, 0.0)
        chosen = pick(lon_ref[...], now - before)
        for way in range(2):
            halo_copy(number, way).wait_recv()
        u = dot(chosen, hist[number])
        if decoder:
            u = ((u + aside) * 0.5).astype(BF).astype(F32)
        gain_a = side([tile[0:1] + tile[2:3] + tile[4:5], tile[1:2] + tile[3:4] + tile[5:6]])
        gain_b = side([tile[6:7] + tile[8:9] + tile[10:11], tile[7:8] + tile[9:10] + tile[11:12]])

        def strip(j):
            start = STRIP * j if j < 9 else HALF + STRIP * (j - 9)
            return packs[number, start : start + STRIP, :]

        def bias(j):
            start = HALF_W + TOK * j if j < 4 else HALF + HALF_W + TOK * (j - 4)
            return packs[number, start : start + TOK, :]

        hist[number + 1, TOK : 2 * TOK] = section(u, strip, bias, gain_a, gain_b)
        for way in range(2):
            halo_copy(number + 1, way).start()

    lax.fori_loop(0, 9, lambda i, c: (step(i, False), c)[1], 0)
    lax.fori_loop(9, SECTIONS, lambda i, c: (step(i, True), c)[1], 0)

    back = pick(lon_ref[...], -offset(params(SECTIONS - 1)))
    for way in range(2):
        halo_copy(SECTIONS, way).wait_recv()
    final = dot(back, hist[SECTIONS])
    share = WIDTH // SEGS
    for s in range(SEGS):
        pieces[s, :, :share] = final[:, share * s : share * (s + 1)].astype(BF)

    def piece_copy(d):
        there = lax.rem(seg + d, SEGS)
        return pltpu.make_async_remote_copy(
            pieces.at[there],
            received.at[seg],
            f_send.at[d],
            f_recv.at[d],
            device_id=(there, place),
            device_id_type=MESH,
        )

    for d in range(1, SEGS):
        piece_copy(d).start()
    mine = pltpu.make_async_copy(pieces.at[seg], received.at[seg], local_sem.at[0])

    @pl.when(folded)
    def _():
        piece_copy(0).start()

    @pl.when(jnp.logical_not(folded))
    def _():
        mine.start()

    def sent(half):
        for n in (1, 2, 3):
            own_copy(half, n).wait_send()

    sent(1)

    @pl.when(seg >= EARLY)
    def _():
        sent(0)

    @pl.when(seg < EARLY)
    def _():
        for n in range(1, SEGS):
            cut_copy(n).wait_send()

    def early_sent(number, carry):
        @pl.when(seg != number)
        def _():
            for n in range(1, chips):
                spread_copy(number, n).wait_send()
            cross_copy(number, plane).wait_send()

        return carry

    def late_sent(number, carry):
        same = lax.rem(source(number), 2) == column

        @pl.when(same)
        def _():
            facing_copy(number).wait_send()

        @pl.when(jnp.logical_not(same))
        def _():
            cross_copy(number, 1 - plane).wait_send()

        return carry

    lax.fori_loop(0, EARLY, early_sent, 0)
    lax.fori_loop(EARLY, SECTIONS, late_sent, 0)

    @pl.when(folded)
    def _():
        swap_copy.wait_send()

    def finish(number, carry):
        @pl.when((number < SECTIONS) & (source(number) != seg))
        def _():
            sibling_copy(number, core).wait_send()

        for way in range(2):
            halo_copy(number, way).wait_send()
        return carry

    lax.fori_loop(0, SECTIONS + 1, finish, 0)
    for d in range(1, SEGS):
        piece_copy(d).wait()

    @pl.when(folded)
    def _():
        piece_copy(0).wait()

    @pl.when(jnp.logical_not(folded))
    def _():
        mine.wait()

    out_ref[...] = received[...]


def split3(x):
    high = x.astype(BF).astype(F32)
    middle = (x - high).astype(BF).astype(F32)
    return high, middle, x - high - middle


def per_device(
    fields, entry_order, shift_offsets, qkv_weight, out_weight, up_weight, down_weight,
    attn_bias, norm_gain,
):
    dma = pltpu.SemaphoreType.DMA
    vmem = pl.BlockSpec(memory_space=pltpu.VMEM)
    smem = pl.BlockSpec(memory_space=pltpu.SMEM)
    got = pl.pallas_call(
        kernel,
        out_shape=jax.ShapeDtypeStruct((SEGS, TOK, 128), BF),
        in_specs=[vmem, smem, smem, vmem, vmem, vmem, vmem, vmem, vmem],
        out_specs=vmem,
        scratch_shapes=[
            pltpu.VMEM((SECTIONS, PACK, 128), BF),
            pltpu.VMEM((2, PACK, 128), BF),
            pltpu.VMEM((SECTIONS + 1, 3 * TOK, 256), BF),
            pltpu.VMEM((TOK, 128), F32),
            pltpu.VMEM((TOK, 256), F32),
            pltpu.VMEM((TOK, 256), BF),
            pltpu.VMEM((8, 256), F32),
            pltpu.VMEM((SEGS, TOK, 128), BF),
            pltpu.VMEM((SEGS, TOK, 128), BF),
            dma((1,)), dma((2,)), dma((SEGS,)), dma((EARLY,)), dma((EARLY, 8)), dma((EARLY,)),
            dma((SECTIONS,)), dma((SECTIONS,)), dma((SECTIONS,)), dma((SECTIONS,)), dma((2, 4)),
            dma((SECTIONS,)), dma((SECTIONS,)), dma((SECTIONS,)), dma((SECTIONS + 1, 2)), dma((SECTIONS + 1, 2)), dma((SEGS,)),
            dma((SEGS,)),
        ],
        compiler_params=pltpu.CompilerParams(
            collective_id=0, has_side_effects=True, vmem_limit_bytes=56 * 2**20
        ),
        name="sections",
    )(
        fields.reshape(4, 2, 2, 6, LON, WIDTH), entry_order, shift_offsets[:, :, 0],
        qkv_weight[:, 0], out_weight[:, 0], up_weight[:, 0], down_weight[:, 0],
        attn_bias[:, 0], norm_gain[:, 0],
    )
    share = WIDTH // SEGS
    got = got[:, :, :share].reshape(2, 2, 2, 2, 6, LON, share).transpose(0, 2, 3, 1, 4, 5, 6)
    got = got.reshape(4, 2, 12, LON, share)
    chosen = (entry_order[None, :] == jnp.arange(4)[:, None]).astype(jnp.int32)
    place = jnp.sum(chosen * jnp.arange(4)[None, :], axis=1)
    return jnp.take(got, place, axis=0)


def solution(mesh):
    placed = (
        P(None, None, None, "lon", None),
        P(),
        P(None, None, "segment"),
        P(None, "segment", None, None),
        P(None, "segment", None, None),
        P(None, "segment", None, None),
        P(None, "segment", None, None),
        P(None, "segment", None, None, None, None),
        P(None, "segment", None, None),
    )
    return jax.shard_map(
        per_device,
        mesh=mesh,
        in_specs=placed,
        out_specs=P(None, None, None, "lon", "segment"),
        check_vma=False,
    )
```

```python
import functools
import math

import jax
import jax.numpy as jnp
from jax import lax
from jax.experimental import pallas as pl
from jax.experimental.pallas import tpu as pltpu
from jax.sharding import PartitionSpec as P

BF = jnp.bfloat16
F32 = jnp.float32
MESH = pl.DeviceIdType.MESH
NT = (((1,), (1,)), ((), ()))
TN = (((0,), (0,)), ((), ()))
NN = (((1,), (0,)), ((), ()))

SEGS = 8
SECTIONS = 16
EARLY = 3
HEADS = 6
TOK = 144
WIDTH = 192
LON = 12
STRIP = 192
HALF_W = 9 * STRIP
HALF_B = 4 * TOK
HALF = HALF_W + HALF_B
PACK = 2 * HALF
PARAMS = HALF + HALF_W + 3 * TOK
EPS = 1e-5
QSCALE = math.log2(math.e) / math.sqrt(32.0)


def dot(a, b, dims=NN):
    return lax.dot_general(a, b, dims, preferred_element_type=F32)


def side(parts):
    return jnp.concatenate(parts, axis=1)


def down(parts):
    return jnp.concatenate(parts, axis=0)


def lanes(shape):
    return lax.broadcasted_iota(jnp.int32, shape, len(shape) - 1)


def normalize(x, gain, inside):
    mean = jnp.sum(x, axis=-1, keepdims=True) * (1.0 / WIDTH)
    centred = x - mean * inside
    spread = jnp.sum(centred * centred, axis=-1, keepdims=True) * (1.0 / WIDTH)
    return (centred * lax.rsqrt(spread + EPS) * gain).astype(BF)


def pick(token, lon, shift):
    x = lon + shift
    wrap = jnp.where(x < 0, float(LON - TOK), jnp.where(x > LON - 1, float(TOK - LON), 0.0))
    target = token + shift + wrap + float(TOK)
    col = lanes((TOK, 128)).astype(F32)
    tiles = [jnp.where(col + float(128 * j) == target, 1.0, 0.0).astype(BF) for j in range(4)]
    return side(tiles)[:, : 3 * TOK]


def section(u, strip, bias, gain_a, gain_b):
    col = lanes((1, 256))
    inside = jnp.where(col < WIDTH, 1.0, 0.0)
    low = jnp.where(lanes((1, 128)) < 64, 1.0, 0.0)
    normed = normalize(u, gain_a, inside)
    short = normed[:, :WIDTH]
    qk = dot(short, side([strip(0), strip(1), strip(2)]))
    qb = (qk[:, :256] * QSCALE).astype(BF)
    kb = side([qk[:, 256:], pltpu.roll(qk[:, 128:256], 64, 1)]).astype(BF)
    mixed = strip(4)
    vt = dot(side([strip(3), mixed]), normed, NT).astype(BF)
    zero = jnp.zeros((TOK, 256), BF)
    pos = lanes((TOK, 256))
    spread_q = down(
        [jnp.where((pos >= 32 * h) & (pos < 32 * h + 32), qb, zero) for h in range(HEADS)]
        + [jnp.zeros((32, 256), BF)]
    )
    scores = dot(kb, spread_q, NT) + side([bias(j) for j in range(7)]).astype(F32)
    top = jnp.max(scores, axis=0, keepdims=True)
    expo = jnp.exp2(scores - top)
    inverse = 1.0 / jnp.sum(expo, axis=0, keepdims=True)
    expo = expo.astype(BF)
    parts = []
    for h in range(HEADS):
        cut = slice(128 * h, 128 * h + 256)
        part = dot(vt[32 * h : 32 * h + 32], expo[:, cut]) * inverse[:, cut]
        if h:
            part = pltpu.roll(part, 256 - 16 * h, 1)
        parts.append(part[:, :TOK])
    context = down(parts).astype(BF)
    out = dot(context, side([strip(5), mixed]), TN)
    out = side([out[:, :128], pltpu.roll(out[:, 128:], 64, 1) * low])
    x1 = u + out.astype(BF).astype(F32)
    normed = normalize(x1, gain_b, inside)[:, :WIDTH]
    hidden = jax.nn.gelu(dot(normed, side([strip(6 + j) for j in range(6)]))).astype(BF)
    low_t = down([side([strip(12 + j) for j in range(6)]), jnp.zeros((64, 768), BF)])
    y = dot(hidden, low_t, NT)
    return (x1 + y).astype(BF)


def kernel(
    fields_ref, order_ref, shift_ref, qkv_ref, out_w_ref, up_ref, low_ref, bias_ref, gain_ref,
    out_ref,
    packs, other, hist, token_ref, lon_ref, stage, swap, gains, pieces, received,
    local_sem, swap_sem, a_send, a_recv, b_send, b_recv, x_send, x_recv,
    c_send, c_recv, w_send, w_recv, s_send, s_recv, h_send, h_recv, f_send, f_recv,
):
    seg = lax.axis_index("segment")
    me = lax.axis_index("lon")
    ring = lax.axis_size("lon")
    half_ring = ring // 2
    core = lax.rem(me, 2)
    sibling = me + 1 - 2 * core
    column = lax.rem(seg, 2)
    facing = seg + 1 - 2 * column
    slot = column + 2 * (seg // 4)
    lat = lax.rem(seg // 2, 2)
    across = lax.rem(me + half_ring, ring)
    folded = me >= half_ring

    def along(place):
        place = lax.rem(place + ring, ring)
        return jnp.where(place < half_ring, place, 3 * half_ring - 1 - place)

    place = along(me)
    west, east = along(place - 1), along(place + 1)

    barrier = pltpu.get_barrier_semaphore()

    def greet(seg_to, lon_to):
        pl.semaphore_signal(barrier, inc=1, device_id=(seg_to, lon_to), device_id_type=MESH)

    for d in (2, 4, 6):
        greet(lax.rem(seg + d, SEGS), me)
    greet(facing, across)
    greet(seg, west)
    greet(seg, east)
    for d in range(1, SEGS):
        greet(lax.rem(seg + d, SEGS), place)
    greet(seg, jnp.where(folded, place, sibling))
    chips = half_ring // 2
    chip = lax.rem(me, half_ring) // 2
    plane = me // half_ring

    def on_chip(n):
        return plane * half_ring + 2 * lax.rem(chip + n, chips) + core

    for n in range(1, chips):
        greet(seg, on_chip(n))
    greet(seg, across)
    for n in range(1, 4):
        greet(lax.rem(facing + 2 * n, SEGS), across)

    def source(number):
        return jnp.minimum(number, SECTIONS - 1 - number)

    def own_number(half):
        return seg if half == 0 else SECTIONS - 1 - seg

    def prepare(half):
        number = own_number(half)

        def put(start, block):
            block = block.astype(BF)
            packs[number, start : start + block.shape[0], :] = block
            other[half, start : start + block.shape[0], :] = block

        def put_strip(j, block):
            put(STRIP * j if j < 9 else HALF + STRIP * (j - 9), block)

        low = lanes((STRIP, 128)) < 64
        qkv = [qkv_ref[half, :, 128 * j : 128 * j + 128].astype(F32) for j in range(4)]
        put_strip(0, qkv[0])
        put_strip(1, jnp.where(low, qkv[1], qkv[2]))
        put_strip(2, jnp.where(low, pltpu.roll(qkv[1], 64, 1), pltpu.roll(qkv[2], 64, 1)))
        eye = (lax.broadcasted_iota(jnp.int32, (WIDTH, WIDTH), 0) == lanes((WIDTH, WIDTH)))
        turned = dot(jnp.where(eye, 1.0, 0.0).astype(BF), qkv_ref[half, :, 384:576], NT)
        out_w = out_w_ref[half].astype(F32)
        put_strip(3, turned[:, :128])
        put_strip(4, side([turned[:, 128:], out_w[:, 128:]]))
        put_strip(5, out_w[:, :128])
        for j in range(6):
            put_strip(6 + j, up_ref[half, :, 128 * j : 128 * j + 128])
            put_strip(12 + j, low_ref[half, :, 128 * j : 128 * j + 128])

        eye = (lax.broadcasted_iota(jnp.int32, (TOK, TOK), 0) == lanes((TOK, TOK)))
        eye = jnp.where(eye, 1.0, 0.0).astype(BF)

        def put_bias(window, store):
            table = bias_ref[half, window].reshape(HEADS * TOK, TOK)
            top = jnp.max(table, axis=-1, keepdims=True)
            table = ((table - top) * math.log2(math.e)).astype(BF)
            table = dot(eye, down([table, jnp.zeros((32, TOK), BF)]), NT).astype(BF)
            for j in range(7):
                start = HALF_W + TOK * j if j < 4 else HALF + HALF_W + TOK * (j - 4)
                store(start, table[:, 128 * j : 128 * j + 128])

        def store_own(start, block):
            packs[number, start : start + TOK, :] = block

        def store_other(start, block):
            other[half, start : start + TOK, :] = block

        put_bias(lat, store_own)
        put_bias(1 - lat, store_other)
        gains[...] = jnp.zeros_like(gains)
        gains[0:2, :WIDTH] = gain_ref[half]
        rows = []
        for n in range(2):
            for part in split3(gains[n : n + 1, :]):
                rows += [part[:, :128], part[:, 128:]]
        rows += [jnp.full((1, 128), shift_ref[half, 0, t].astype(F32)) for t in range(4)]
        put(PARAMS, down(rows))
        rest = jnp.zeros((TOK - 16, 128), BF)
        put(PARAMS + 16, rest)

    half_rows = pl.ds(pl.multiple_of(core * HALF, 16), HALF)

    def part_rows(plane_of):
        start = core * HALF + plane_of * (HALF // 2)
        return pl.ds(pl.multiple_of(start, 16), HALF // 2)

    def own_copy(half, n):
        number = own_number(half)
        ref = packs.at[number] if n == 2 else other.at[half]
        return pltpu.make_async_remote_copy(
            ref.at[half_rows], packs.at[number, half_rows], w_send.at[half, n], w_recv.at[number],
            device_id=(lax.rem(seg + 2 * n, SEGS), me), device_id_type=MESH,
        )

    def send_weights(half):
        facing_copy(own_number(half)).start()
        for n in (1, 3, 2):
            own_copy(half, n).start()

    def facing_copy(number):
        rows = part_rows(plane)
        return pltpu.make_async_remote_copy(
            packs.at[number, rows], packs.at[number, rows], c_send.at[number], c_recv.at[number],
            device_id=(facing, across), device_id_type=MESH,
        )

    def cross_copy(number, plane_of):
        rows = part_rows(plane_of)
        return pltpu.make_async_remote_copy(
            packs.at[number, rows], packs.at[number, rows], x_send.at[number], x_recv.at[number],
            device_id=(seg, across), device_id_type=MESH,
        )

    def sibling_copy(number, start):
        start = pl.multiple_of(start * HALF, 16)
        return pltpu.make_async_remote_copy(
            packs.at[number, pl.ds(start, HALF)],
            packs.at[number, pl.ds(start, HALF)],
            s_send.at[number],
            s_recv.at[number],
            device_id=(seg, sibling),
            device_id_type=MESH,
        )

    def first(number):
        seg_of = source(number)

        @pl.when((seg_of != seg) & (lax.rem(seg_of, 2) == column))
        def _():
            pltpu.make_async_remote_copy(
                packs.at[number, half_rows], packs.at[number, half_rows], w_send.at[0, 0],
                w_recv.at[number], device_id=(facing, across), device_id_type=MESH,
            ).wait_recv()
            facing_copy(number).start()
            sibling_copy(number, core).start()

    def second(number):
        @pl.when(lax.rem(source(number), 2) != column)
        def _():
            rows = part_rows(1 - plane)
            pltpu.make_async_remote_copy(
                packs.at[number, rows], packs.at[number, rows], c_send.at[number],
                c_recv.at[number], device_id=(facing, across), device_id_type=MESH,
            ).wait_recv()
            cross_copy(number, 1 - plane).start()

    def third(number):
        @pl.when(lax.rem(source(number), 2) != column)
        def _():
            cross_copy(number, plane).wait_recv()
            sibling_copy(number, core).start()

    cut = HALF // 2 // chips

    def cut_rows(plane_of, chip_of):
        start = core * HALF + plane_of * (HALF // 2) + chip_of * cut
        return pl.ds(pl.multiple_of(start, 16), cut)

    far = chips // 2

    def cut_copy(n, k):
        of = lax.rem(chip + k * far, chips)
        if n < 4:
            seg_to, lon_to, rows = seg + 2 * n, me, cut_rows(plane, of)
        else:
            seg_to, lon_to, rows = facing + 2 * n, across, cut_rows(1 - plane, of)
        ref = other.at[0] if n % 2 else packs.at[seg]
        return pltpu.make_async_remote_copy(
            ref.at[rows], packs.at[seg, rows], a_send.at[n, k], a_recv.at[jnp.minimum(seg, EARLY - 1)],
            device_id=(lax.rem(seg_to, SEGS), lon_to), device_id_type=MESH,
        )

    def send_cuts():
        for n in (4, 1, 3, 5, 7, 2, 6):
            for k in range(2 if chips > 1 else 1):
                cut_copy(n, k).start()

    peers = [n for k in range(1, far) for n in (k, chips - k)]

    def spread_copy(number, n):
        rows = cut_rows(plane, chip)
        return pltpu.make_async_remote_copy(
            packs.at[number, rows], packs.at[number, rows], b_send.at[number, n], b_recv.at[number],
            device_id=(seg, on_chip(n)), device_id_type=MESH,
        )

    def spread(number):
        @pl.when(seg != number)
        def _():
            rows = pl.ds(pl.multiple_of(core * HALF, 16), cut * (2 if chips > 1 else 1))
            pltpu.make_async_remote_copy(
                packs.at[number, rows], packs.at[number, rows], a_send.at[0, 0], a_recv.at[number],
                device_id=(seg, across), device_id_type=MESH,
            ).wait_recv()
            for n in peers:
                spread_copy(number, n).start()

    def cross(number):
        @pl.when(seg != number)
        def _():
            start = core * HALF + plane * (HALF // 2)
            rows = pl.ds(pl.multiple_of(start, 16), max(1, len(peers)) * cut)
            if chips > 1:
                pltpu.make_async_remote_copy(
                    packs.at[number, rows], packs.at[number, rows], b_send.at[number, 0],
                    b_recv.at[number], device_id=(seg, across), device_id_type=MESH,
                ).wait_recv()
            cross_copy(number, plane).start()

    def pair_up(number):
        @pl.when(seg != number)
        def _():
            cross_copy(number, 1 - plane).wait_recv()
            sibling_copy(number, core).start()

    def halo_copy(number, way):
        return pltpu.make_async_remote_copy(
            hist.at[number, pl.ds(TOK, TOK)],
            hist.at[number, pl.ds(2 * TOK if way == 0 else 0, TOK)],
            h_send.at[number, way],
            h_recv.at[number, way],
            device_id=(seg, west if way == 0 else east),
            device_id_type=MESH,
        )

    swap_copy = pltpu.make_async_remote_copy(
        swap, hist.at[0, pl.ds(TOK, TOK)], swap_sem.at[0], swap_sem.at[1],
        device_id=(seg, place), device_id_type=MESH,
    )

    prepare(0)
    stage[...] = jnp.zeros_like(stage)
    micro = order_ref[slot]
    for n in range(6):
        cells = fields_ref[micro, 6 * lat + n].astype(F32)
        for level in range(2):
            start = 72 * level + LON * n
            stage[start : start + LON, :WIDTH] = cells[:, level, :]

    pl.semaphore_wait(barrier, 14 + chips + 3)

    @pl.when(seg < EARLY)
    def _():
        send_cuts()

    @pl.when(seg >= EARLY)
    def _():
        send_weights(0)


    @pl.when(folded)
    def _():
        swap[...] = stage[...].astype(BF)
        swap_copy.start()
        swap_copy.wait_recv()

    @pl.when(jnp.logical_not(folded))
    def _():
        hist[0, TOK : 2 * TOK] = stage[...].astype(BF)

    for way in range(2):
        halo_copy(0, way).start()
    token = lax.broadcasted_iota(jnp.int32, (TOK, 128), 0)
    token_ref[...] = token.astype(F32)
    lon_ref[...] = lax.rem(token, LON).astype(F32)
    spread(0)
    prepare(1)
    cross(0)
    spread(1)
    cross(1)
    spread(2)
    pair_up(0)

    def params(number):
        return packs[number, PARAMS : PARAMS + 16, :].astype(F32)

    def offset(tile):
        row = lax.broadcasted_iota(jnp.int32, (16, 128), 0)
        return jnp.sum(jnp.where(row == 12 + slot, tile, 0.0), axis=0, keepdims=True)

    def step(number, decoder):
        if not decoder:
            @pl.when(number == 0)
            def _():
                @pl.when(seg >= SEGS // 2)
                def _():
                    send_weights(1)

            @pl.when(number == 1)
            def _():
                pair_up(1)
                for n in range(EARLY, 7):
                    first(n)
                cross(2)

            @pl.when(number == 2)
            def _():
                @pl.when(seg < SEGS // 2)
                def _():
                    send_weights(1)

                pair_up(2)
                for n in range(EARLY, 6):
                    second(n)

            @pl.when(number == 3)
            def _():
                third(3)
                third(4)

        @pl.when((number >= 2) & (number < SECTIONS - 5))
        def _():
            first(number + 5)

        @pl.when((number >= 3) & (number < SECTIONS - 3))
        def _():
            second(number + 3)

        @pl.when((number >= 4) & (number < SECTIONS - 1))
        def _():
            third(number + 1)

        @pl.when(source(number) != seg)
        def _():
            sibling_copy(number, 1 - core).wait_recv()

        tile = params(number)
        now = offset(tile)
        if decoder:
            before = offset(params(number - 1))
            earlier = now - offset(params(15 - number))
            aside = dot(pick(token_ref[...], lon_ref[...], earlier), hist[16 - number])
        else:
            before = offset(params(jnp.maximum(number - 1, 0)))
            before = before * jnp.where(number > 0, 1.0, 0.0)
        chosen = pick(token_ref[...], lon_ref[...], now - before)
        for way in range(2):
            halo_copy(number, way).wait_recv()
        u = dot(chosen, hist[number])
        if decoder:
            u = ((u + aside) * 0.5).astype(BF).astype(F32)
        gain_a = side([tile[0:1] + tile[2:3] + tile[4:5], tile[1:2] + tile[3:4] + tile[5:6]])
        gain_b = side([tile[6:7] + tile[8:9] + tile[10:11], tile[7:8] + tile[9:10] + tile[11:12]])

        def strip(j):
            start = STRIP * j if j < 9 else HALF + STRIP * (j - 9)
            return packs[number, start : start + STRIP, :]

        def bias(j):
            start = HALF_W + TOK * j if j < 4 else HALF + HALF_W + TOK * (j - 4)
            return packs[number, start : start + TOK, :]

        hist[number + 1, TOK : 2 * TOK] = section(u, strip, bias, gain_a, gain_b)
        for way in range(2):
            halo_copy(number + 1, way).start()

    lax.fori_loop(0, 9, lambda i, c: (step(i, False), c)[1], 0)
    lax.fori_loop(9, SECTIONS, lambda i, c: (step(i, True), c)[1], 0)

    order = lax.broadcasted_iota(jnp.int32, (TOK, 128), 0)
    lon = lax.rem(order, 24) // 2
    token = (lax.rem(order, 2) * 6 + order // 24) * LON + lon
    back = pick(token.astype(F32), lon.astype(F32), -offset(params(SECTIONS - 1)))
    for way in range(2):
        halo_copy(SECTIONS, way).wait_recv()
    final = dot(back, hist[SECTIONS])
    share = WIDTH // SEGS
    for s in range(SEGS):
        pieces[s, :, :share] = final[:, share * s : share * (s + 1)].astype(BF)

    def piece_copy(d):
        there = lax.rem(seg + d, SEGS)
        return pltpu.make_async_remote_copy(
            pieces.at[there],
            received.at[seg],
            f_send.at[d],
            f_recv.at[d],
            device_id=(there, place),
            device_id_type=MESH,
        )

    for d in range(1, SEGS):
        piece_copy(d).start()
    mine = pltpu.make_async_copy(pieces.at[seg], received.at[seg], local_sem.at[0])

    @pl.when(folded)
    def _():
        piece_copy(0).start()

    @pl.when(jnp.logical_not(folded))
    def _():
        mine.start()

    def sent(half):
        for n in (1, 2, 3):
            own_copy(half, n).wait_send()

    sent(1)

    @pl.when(seg >= EARLY)
    def _():
        sent(0)

    @pl.when(seg < EARLY)
    def _():
        for n in range(1, SEGS):
            for k in range(2 if chips > 1 else 1):
                cut_copy(n, k).wait_send()

    def early_sent(number, carry):
        @pl.when(seg != number)
        def _():
            for n in peers:
                spread_copy(number, n).wait_send()
            cross_copy(number, plane).wait_send()

        return carry

    def late_sent(number, carry):
        same = lax.rem(source(number), 2) == column

        @pl.when(same)
        def _():
            facing_copy(number).wait_send()

        @pl.when(jnp.logical_not(same))
        def _():
            cross_copy(number, 1 - plane).wait_send()

        return carry

    lax.fori_loop(0, EARLY, early_sent, 0)
    lax.fori_loop(EARLY, SECTIONS, late_sent, 0)

    @pl.when(folded)
    def _():
        swap_copy.wait_send()

    def finish(number, carry):
        @pl.when((number < SECTIONS) & (source(number) != seg))
        def _():
            sibling_copy(number, core).wait_send()

        for way in range(2):
            halo_copy(number, way).wait_send()
        return carry

    lax.fori_loop(0, SECTIONS + 1, finish, 0)
    for d in range(1, SEGS):
        piece_copy(d).wait()

    @pl.when(folded)
    def _():
        piece_copy(0).wait()

    @pl.when(jnp.logical_not(folded))
    def _():
        mine.wait()

    for m in range(4):
        at = jnp.int32(0)
        for t in range(1, 4):
            at = jnp.where(order_ref[t] == m, 4 * (t // 2) + t % 2, at)
        for a in range(2):
            out_ref[m, a] = received[at + 2 * a]


def split3(x):
    high = x.astype(BF).astype(F32)
    middle = (x - high).astype(BF).astype(F32)
    return high, middle, x - high - middle


def per_device(
    fields, entry_order, shift_offsets, qkv_weight, out_weight, up_weight, down_weight,
    attn_bias, norm_gain,
):
    dma = pltpu.SemaphoreType.DMA
    vmem = pl.BlockSpec(memory_space=pltpu.VMEM)
    smem = pl.BlockSpec(memory_space=pltpu.SMEM)
    got = pl.pallas_call(
        kernel,
        out_shape=jax.ShapeDtypeStruct((4, 2, TOK, 128), BF),
        in_specs=[vmem, smem, smem, vmem, vmem, vmem, vmem, vmem, vmem],
        out_specs=vmem,
        scratch_shapes=[
            pltpu.VMEM((SECTIONS, PACK, 128), BF),
            pltpu.VMEM((2, PACK, 128), BF),
            pltpu.VMEM((SECTIONS + 1, 3 * TOK, 256), BF),
            pltpu.VMEM((TOK, 128), F32),
            pltpu.VMEM((TOK, 128), F32),
            pltpu.VMEM((TOK, 256), F32),
            pltpu.VMEM((TOK, 256), BF),
            pltpu.VMEM((8, 256), F32),
            pltpu.VMEM((SEGS, TOK, 128), BF),
            pltpu.VMEM((SEGS, TOK, 128), BF),
            dma((1,)), dma((2,)), dma((SEGS, 2)), dma((EARLY,)), dma((EARLY, 8)), dma((EARLY,)),
            dma((SECTIONS,)), dma((SECTIONS,)), dma((SECTIONS,)), dma((SECTIONS,)), dma((2, 4)),
            dma((SECTIONS,)), dma((SECTIONS,)), dma((SECTIONS,)), dma((SECTIONS + 1, 2)), dma((SECTIONS + 1, 2)), dma((SEGS,)),
            dma((SEGS,)),
        ],
        compiler_params=pltpu.CompilerParams(
            collective_id=0, has_side_effects=True, vmem_limit_bytes=56 * 2**20
        ),
        name="sections",
    )(
        fields.transpose(0, 2, 3, 1, 4), entry_order, shift_offsets.transpose(1, 2, 0),
        qkv_weight[:, 0], out_weight[:, 0], up_weight[:, 0], down_weight[:, 0].swapaxes(1, 2),
        attn_bias[:, 0], norm_gain[:, 0],
    )
    share = WIDTH // SEGS
    got = got[..., :share].reshape(4, 12, LON, 2, share)
    return got.transpose(0, 3, 1, 2, 4)


def solution(mesh):
    placed = (
        P(None, None, None, "lon", None),
        P(),
        P(None, None, "segment"),
        P(None, "segment", None, None),
        P(None, "segment", None, None),
        P(None, "segment", None, None),
        P(None, "segment", None, None),
        P(None, "segment", None, None, None, None),
        P(None, "segment", None, None),
    )
    return jax.shard_map(
        per_device,
        mesh=mesh,
        in_specs=placed,
        out_specs=P(None, None, None, "lon", "segment"),
        check_vma=False,
    )
```

```python
import functools
import math

import jax
import jax.numpy as jnp
from jax import lax
from jax.experimental import pallas as pl
from jax.experimental.pallas import tpu as pltpu
from jax.sharding import PartitionSpec as P

BF = jnp.bfloat16
F32 = jnp.float32
MESH = pl.DeviceIdType.MESH
NT = (((1,), (1,)), ((), ()))
TN = (((0,), (0,)), ((), ()))
NN = (((1,), (0,)), ((), ()))

SEGS = 8
SECTIONS = 16
EARLY = 3
HEADS = 6
TOK = 144
WIDTH = 192
LON = 12
STRIP = 192
HALF_W = 9 * STRIP
HALF_B = 4 * TOK
HALF = HALF_W + HALF_B
PACK = 2 * HALF
ROWS = TOK // 3
PARAMS = HALF + HALF_W + 3 * TOK
EPS = 1e-5
QSCALE = math.log2(math.e) / math.sqrt(32.0)


def dot(a, b, dims=NN):
    return lax.dot_general(a, b, dims, preferred_element_type=F32)


def side(parts):
    return jnp.concatenate(parts, axis=1)


def down(parts):
    return jnp.concatenate(parts, axis=0)


def lanes(shape):
    return lax.broadcasted_iota(jnp.int32, shape, len(shape) - 1)


def normalize(x, gain, inside):
    mean = jnp.sum(x, axis=-1, keepdims=True) * (1.0 / WIDTH)
    centred = x - mean * inside
    spread = jnp.sum(centred * centred, axis=-1, keepdims=True) * (1.0 / WIDTH)
    return (centred * lax.rsqrt(spread + EPS) * gain).astype(BF)


def pick(token, lon, shift):
    x = lon + shift
    wrap = jnp.where(x < 0, float(LON - TOK), jnp.where(x > LON - 1, float(TOK - LON), 0.0))
    target = token + shift + wrap + float(TOK)
    col = lanes((TOK, 128)).astype(F32)
    tiles = [jnp.where(col + float(128 * j) == target, 1.0, 0.0).astype(BF) for j in range(4)]
    return side(tiles)[:, : 3 * TOK]


def section(u, strip, bias, gain_a, gain_b):
    col = lanes((1, 256))
    inside = jnp.where(col < WIDTH, 1.0, 0.0)
    low = jnp.where(lanes((1, 128)) < 64, 1.0, 0.0)
    normed = normalize(u, gain_a, inside)
    short = normed[:, :WIDTH]
    qk = dot(short, side([strip(0), strip(1), strip(2)]))
    qb = (qk[:, :256] * QSCALE).astype(BF)
    kb = side([qk[:, 256:], pltpu.roll(qk[:, 128:256], 64, 1)]).astype(BF)
    mixed = strip(4)
    vt = dot(side([strip(3), mixed]), normed, NT).astype(BF)
    zero = jnp.zeros((TOK, 256), BF)
    pos = lanes((TOK, 256))
    spread_q = down(
        [jnp.where((pos >= 32 * h) & (pos < 32 * h + 32), qb, zero) for h in range(HEADS)]
        + [jnp.zeros((32, 256), BF)]
    )
    scores = dot(kb, spread_q, NT) + side([bias(j) for j in range(7)]).astype(F32)
    top = jnp.max(scores, axis=0, keepdims=True)
    expo = jnp.exp2(scores - top)
    inverse = 1.0 / jnp.sum(expo, axis=0, keepdims=True)
    expo = expo.astype(BF)
    parts = []
    for h in range(HEADS):
        cut = slice(128 * h, 128 * h + 256)
        part = dot(vt[32 * h : 32 * h + 32], expo[:, cut]) * inverse[:, cut]
        if h:
            part = pltpu.roll(part, 256 - 16 * h, 1)
        parts.append(part[:, :TOK])
    context = down(parts).astype(BF)
    out = dot(context, side([strip(5), mixed]), TN)
    out = side([out[:, :128], pltpu.roll(out[:, 128:], 64, 1) * low])
    x1 = u + out.astype(BF).astype(F32)
    normed = normalize(x1, gain_b, inside)[:, :WIDTH]
    hidden = jax.nn.gelu(dot(normed, side([strip(6 + j) for j in range(6)]))).astype(BF)
    low_t = down([side([strip(12 + j) for j in range(6)]), jnp.zeros((64, 768), BF)])
    y = dot(hidden, low_t, NT)
    return (x1 + y).astype(BF)


def kernel(
    order_ref, shift_ref, gain_ref, *refs,
):
    given, out_ref, held, rest = refs[:6], refs[6], refs[7:13], refs[13:]
    fields_ref, qkv_ref, out_w_ref, up_ref, low_ref, bias_ref = held
    (
        packs, other, hist, token_ref, lon_ref, share_ref, stage, swap, gains, pieces, received,
        local_sem, swap_sem, a_send, a_recv, b_send, b_recv, x_send, x_recv,
        c_send, c_recv, w_send, w_recv, s_send, s_recv, h_send, h_recv, f_send, f_recv,
        in_sem,
    ) = rest
    seg = lax.axis_index("segment")
    me = lax.axis_index("lon")
    ring = lax.axis_size("lon")
    half_ring = ring // 2
    core = lax.rem(me, 2)
    sibling = me + 1 - 2 * core
    column = lax.rem(seg, 2)
    facing = seg + 1 - 2 * column
    slot = column + 2 * (seg // 4)
    lat = lax.rem(seg // 2, 2)
    across = lax.rem(me + half_ring, ring)
    folded = me >= half_ring

    def along(place):
        place = lax.rem(place + ring, ring)
        return jnp.where(place < half_ring, place, 3 * half_ring - 1 - place)

    place = along(me)
    west, east = along(place - 1), along(place + 1)

    def arrival(n, half):
        if n == 0:
            return pltpu.make_async_copy(given[0], held[0], in_sem.at[n, half])
        return pltpu.make_async_copy(given[n].at[half], held[n].at[half], in_sem.at[n, half])

    barrier = pltpu.get_barrier_semaphore()

    def greet(seg_to, lon_to):
        pl.semaphore_signal(barrier, inc=1, device_id=(seg_to, lon_to), device_id_type=MESH)

    for d in (2, 4, 6):
        greet(lax.rem(seg + d, SEGS), me)
    greet(facing, across)
    greet(seg, west)
    greet(seg, east)
    for d in range(1, SEGS):
        greet(lax.rem(seg + d, SEGS), place)
    greet(seg, jnp.where(folded, place, sibling))
    chips = half_ring // 2
    chip = lax.rem(me, half_ring) // 2
    plane = me // half_ring

    def on_chip(n):
        return plane * half_ring + 2 * lax.rem(chip + n, chips) + core

    for n in range(1, chips):
        greet(seg, on_chip(n))
    greet(seg, across)
    for n in range(1, 4):
        greet(lax.rem(facing + 2 * n, SEGS), across)

    for n in (5, 1, 2, 3, 4, 0):
        arrival(n, 0).start()
    for n in range(1, 6):
        arrival(n, 1).start()

    def source(number):
        return jnp.minimum(number, SECTIONS - 1 - number)

    def own_number(half):
        return seg if half == 0 else SECTIONS - 1 - seg

    def prepare(half):
        number = own_number(half)
        for n in range(1, 6):
            arrival(n, half).wait()

        def put(start, block):
            block = block.astype(BF)
            packs[number, start : start + block.shape[0], :] = block
            other[half, start : start + block.shape[0], :] = block

        def put_strip(j, block):
            put(STRIP * j if j < 9 else HALF + STRIP * (j - 9), block)

        low = lanes((STRIP, 128)) < 64
        qkv = [qkv_ref[half, :, 128 * j : 128 * j + 128].astype(F32) for j in range(4)]
        put_strip(0, qkv[0])
        put_strip(1, jnp.where(low, qkv[1], qkv[2]))
        put_strip(2, jnp.where(low, pltpu.roll(qkv[1], 64, 1), pltpu.roll(qkv[2], 64, 1)))
        eye = (lax.broadcasted_iota(jnp.int32, (WIDTH, WIDTH), 0) == lanes((WIDTH, WIDTH)))
        turned = dot(jnp.where(eye, 1.0, 0.0).astype(BF), qkv_ref[half, :, 384:576], NT)
        out_w = out_w_ref[half].astype(F32)
        put_strip(3, turned[:, :128])
        put_strip(4, side([turned[:, 128:], out_w[:, 128:]]))
        put_strip(5, out_w[:, :128])
        for j in range(6):
            put_strip(6 + j, up_ref[half, :, 128 * j : 128 * j + 128])
            put_strip(12 + j, low_ref[half, :, 128 * j : 128 * j + 128])

        eye = (lax.broadcasted_iota(jnp.int32, (TOK, TOK), 0) == lanes((TOK, TOK)))
        eye = jnp.where(eye, 1.0, 0.0).astype(BF)

        def put_bias(window, store):
            table = bias_ref[half, window].reshape(HEADS * TOK, TOK)
            top = jnp.max(table, axis=-1, keepdims=True)
            table = ((table - top) * math.log2(math.e)).astype(BF)
            table = dot(eye, down([table, jnp.zeros((32, TOK), BF)]), NT).astype(BF)
            for j in range(7):
                start = HALF_W + TOK * j if j < 4 else HALF + HALF_W + TOK * (j - 4)
                store(start, table[:, 128 * j : 128 * j + 128])

        def store_own(start, block):
            packs[number, start : start + TOK, :] = block

        def store_other(start, block):
            other[half, start : start + TOK, :] = block

        put_bias(lat, store_own)
        put_bias(1 - lat, store_other)
        gains[...] = jnp.zeros_like(gains)
        gains[0:2, :WIDTH] = gain_ref[half]
        rows = []
        for n in range(2):
            for part in split3(gains[n : n + 1, :]):
                rows += [part[:, :128], part[:, 128:]]
        rows += [jnp.full((1, 128), shift_ref[half, 0, t].astype(F32)) for t in range(4)]
        put(PARAMS, down(rows))
        rest = jnp.zeros((TOK - 16, 128), BF)
        put(PARAMS + 16, rest)

    half_rows = pl.ds(pl.multiple_of(core * HALF, 16), HALF)

    def part_rows(plane_of):
        start = core * HALF + plane_of * (HALF // 2)
        return pl.ds(pl.multiple_of(start, 16), HALF // 2)

    def own_copy(half, n):
        number = own_number(half)
        ref = packs.at[number] if n == 2 else other.at[half]
        return pltpu.make_async_remote_copy(
            ref.at[half_rows], packs.at[number, half_rows], w_send.at[half, n], w_recv.at[number],
            device_id=(lax.rem(seg + 2 * n, SEGS), me), device_id_type=MESH,
        )

    def send_weights(half):
        facing_copy(own_number(half)).start()
        for n in (1, 3, 2):
            own_copy(half, n).start()

    def facing_copy(number):
        rows = part_rows(plane)
        return pltpu.make_async_remote_copy(
            packs.at[number, rows], packs.at[number, rows], c_send.at[number], c_recv.at[number],
            device_id=(facing, across), device_id_type=MESH,
        )

    def cross_copy(number, plane_of):
        rows = part_rows(plane_of)
        return pltpu.make_async_remote_copy(
            packs.at[number, rows], packs.at[number, rows], x_send.at[number], x_recv.at[number],
            device_id=(seg, across), device_id_type=MESH,
        )

    def sibling_copy(number, start):
        start = pl.multiple_of(start * HALF, 16)
        return pltpu.make_async_remote_copy(
            packs.at[number, pl.ds(start, HALF)],
            packs.at[number, pl.ds(start, HALF)],
            s_send.at[number],
            s_recv.at[number],
            device_id=(seg, sibling),
            device_id_type=MESH,
        )

    def first(number):
        seg_of = source(number)

        @pl.when((seg_of != seg) & (lax.rem(seg_of, 2) == column))
        def _():
            pltpu.make_async_remote_copy(
                packs.at[number, half_rows], packs.at[number, half_rows], w_send.at[0, 0],
                w_recv.at[number], device_id=(facing, across), device_id_type=MESH,
            ).wait_recv()
            facing_copy(number).start()
            sibling_copy(number, core).start()

    def second(number):
        @pl.when(lax.rem(source(number), 2) != column)
        def _():
            rows = part_rows(1 - plane)
            pltpu.make_async_remote_copy(
                packs.at[number, rows], packs.at[number, rows], c_send.at[number],
                c_recv.at[number], device_id=(facing, across), device_id_type=MESH,
            ).wait_recv()
            cross_copy(number, 1 - plane).start()

    def third(number):
        @pl.when(lax.rem(source(number), 2) != column)
        def _():
            cross_copy(number, plane).wait_recv()
            sibling_copy(number, core).start()

    cut = HALF // 2 // chips

    def cut_rows(plane_of, chip_of):
        start = core * HALF + plane_of * (HALF // 2) + chip_of * cut
        return pl.ds(pl.multiple_of(start, 16), cut)

    far = chips // 2

    def cut_copy(n, k):
        of = lax.rem(chip + k * far, chips)
        if n < 4:
            seg_to, lon_to, rows = seg + 2 * n, me, cut_rows(plane, of)
        else:
            seg_to, lon_to, rows = facing + 2 * n, across, cut_rows(1 - plane, of)
        ref = other.at[0] if n % 2 else packs.at[seg]
        return pltpu.make_async_remote_copy(
            ref.at[rows], packs.at[seg, rows], a_send.at[n, k], a_recv.at[jnp.minimum(seg, EARLY - 1)],
            device_id=(lax.rem(seg_to, SEGS), lon_to), device_id_type=MESH,
        )

    def send_cuts():
        for n in (4, 1, 3, 5, 7, 2, 6):
            for k in range(2 if chips > 1 else 1):
                cut_copy(n, k).start()

    peers = [n for k in range(1, far) for n in (k, chips - k)]

    def spread_copy(number, n):
        rows = cut_rows(plane, chip)
        return pltpu.make_async_remote_copy(
            packs.at[number, rows], packs.at[number, rows], b_send.at[number, n], b_recv.at[number],
            device_id=(seg, on_chip(n)), device_id_type=MESH,
        )

    def spread(number):
        @pl.when(seg != number)
        def _():
            rows = pl.ds(pl.multiple_of(core * HALF, 16), cut * (2 if chips > 1 else 1))
            pltpu.make_async_remote_copy(
                packs.at[number, rows], packs.at[number, rows], a_send.at[0, 0], a_recv.at[number],
                device_id=(seg, across), device_id_type=MESH,
            ).wait_recv()
            for n in peers:
                spread_copy(number, n).start()

    def cross(number):
        @pl.when(seg != number)
        def _():
            start = core * HALF + plane * (HALF // 2)
            rows = pl.ds(pl.multiple_of(start, 16), max(1, len(peers)) * cut)
            if chips > 1:
                pltpu.make_async_remote_copy(
                    packs.at[number, rows], packs.at[number, rows], b_send.at[number, 0],
                    b_recv.at[number], device_id=(seg, across), device_id_type=MESH,
                ).wait_recv()
            cross_copy(number, plane).start()

    def pair_up(number):
        @pl.when(seg != number)
        def _():
            cross_copy(number, 1 - plane).wait_recv()
            sibling_copy(number, core).start()

    def halo_copy(number, way):
        return pltpu.make_async_remote_copy(
            hist.at[number, pl.ds(TOK, TOK)],
            hist.at[number, pl.ds(2 * TOK if way == 0 else 0, TOK)],
            h_send.at[number, way],
            h_recv.at[number, way],
            device_id=(seg, west if way == 0 else east),
            device_id_type=MESH,
        )

    swap_copy = pltpu.make_async_remote_copy(
        swap, hist.at[0, pl.ds(TOK, TOK)], swap_sem.at[0], swap_sem.at[1],
        device_id=(seg, place), device_id_type=MESH,
    )

    prepare(0)
    stage[...] = jnp.zeros_like(stage)
    arrival(0, 0).wait()
    micro = order_ref[slot]
    for n in range(6):
        cells = fields_ref[micro, 6 * lat + n].astype(F32)
        for level in range(2):
            start = 72 * level + LON * n
            stage[start : start + LON, :WIDTH] = cells[:, level, :]

    pl.semaphore_wait(barrier, 14 + chips + 3)

    @pl.when(seg < EARLY)
    def _():
        send_cuts()

    @pl.when(seg >= EARLY)
    def _():
        send_weights(0)


    @pl.when(folded)
    def _():
        swap[...] = stage[...].astype(BF)
        swap_copy.start()
        swap_copy.wait_recv()

    @pl.when(jnp.logical_not(folded))
    def _():
        hist[0, TOK : 2 * TOK] = stage[...].astype(BF)

    for way in range(2):
        halo_copy(0, way).start()
    token = lax.broadcasted_iota(jnp.int32, (TOK, 128), 0)
    token_ref[...] = token.astype(F32)
    share = WIDTH // SEGS
    feature = lax.broadcasted_iota(jnp.int32, (256, 128), 0)
    for g in range(3):
        lane = lanes((256, 128)) - 32 * g
        inside = (lane >= 0) & (lane < share)
        for s in range(SEGS):
            hit = inside & (feature == lane + share * s)
            share_ref[256 * g : 256 * g + 256, 128 * s : 128 * s + 128] = jnp.where(
                hit, 1.0, 0.0
            ).astype(BF)
    lon_ref[...] = lax.rem(token, LON).astype(F32)
    spread(0)
    prepare(1)
    cross(0)
    spread(1)
    cross(1)
    spread(2)
    pair_up(0)

    def params(number):
        return packs[number, PARAMS : PARAMS + 16, :].astype(F32)

    def offset(tile):
        row = lax.broadcasted_iota(jnp.int32, (16, 128), 0)
        return jnp.sum(jnp.where(row == 12 + slot, tile, 0.0), axis=0, keepdims=True)

    def step(number, decoder):
        if not decoder:
            @pl.when(number == 0)
            def _():
                @pl.when(seg >= SEGS // 2)
                def _():
                    send_weights(1)

            @pl.when(number == 1)
            def _():
                pair_up(1)
                for n in range(EARLY, 7):
                    first(n)
                cross(2)

            @pl.when(number == 2)
            def _():
                @pl.when(seg < SEGS // 2)
                def _():
                    send_weights(1)

                pair_up(2)
                for n in range(EARLY, 6):
                    second(n)

            @pl.when(number == 3)
            def _():
                third(3)
                third(4)

        @pl.when((number >= 2) & (number < SECTIONS - 5))
        def _():
            first(number + 5)

        @pl.when((number >= 3) & (number < SECTIONS - 3))
        def _():
            second(number + 3)

        @pl.when((number >= 4) & (number < SECTIONS - 1))
        def _():
            third(number + 1)

        @pl.when(source(number) != seg)
        def _():
            sibling_copy(number, 1 - core).wait_recv()

        tile = params(number)
        now = offset(tile)
        if decoder:
            before = offset(params(number - 1))
            earlier = now - offset(params(15 - number))
            aside = dot(pick(token_ref[...], lon_ref[...], earlier), hist[16 - number])
        else:
            before = offset(params(jnp.maximum(number - 1, 0)))
            before = before * jnp.where(number > 0, 1.0, 0.0)
        chosen = pick(token_ref[...], lon_ref[...], now - before)
        for way in range(2):
            halo_copy(number, way).wait_recv()
        u = dot(chosen, hist[number])
        if decoder:
            u = ((u + aside) * 0.5).astype(BF).astype(F32)
        gain_a = side([tile[0:1] + tile[2:3] + tile[4:5], tile[1:2] + tile[3:4] + tile[5:6]])
        gain_b = side([tile[6:7] + tile[8:9] + tile[10:11], tile[7:8] + tile[9:10] + tile[11:12]])

        def strip(j):
            start = STRIP * j if j < 9 else HALF + STRIP * (j - 9)
            return packs[number, start : start + STRIP, :]

        def bias(j):
            start = HALF_W + TOK * j if j < 4 else HALF + HALF_W + TOK * (j - 4)
            return packs[number, start : start + TOK, :]

        hist[number + 1, TOK : 2 * TOK] = section(u, strip, bias, gain_a, gain_b)
        for way in range(2):
            halo_copy(number + 1, way).start()

    lax.fori_loop(0, 9, lambda i, c: (step(i, False), c)[1], 0)
    lax.fori_loop(9, SECTIONS, lambda i, c: (step(i, True), c)[1], 0)

    order = lax.broadcasted_iota(jnp.int32, (TOK, 128), 0)
    lon = lax.rem(order, 24) // 2
    token = (lax.rem(order, 2) * 6 + order // 24) * LON + lon
    back = pick(token.astype(F32), lon.astype(F32), -offset(params(SECTIONS - 1)))
    for way in range(2):
        halo_copy(SECTIONS, way).wait_recv()
    final = dot(back, hist[SECTIONS]).astype(BF)
    final = side([final[ROWS * g : ROWS * g + ROWS] for g in range(3)])
    final = dot(final, share_ref[...]).astype(BF)
    for s in range(SEGS):
        pieces[s] = final[:, 128 * s : 128 * s + 128]

    def piece_copy(d):
        there = lax.rem(seg + d, SEGS)
        return pltpu.make_async_remote_copy(
            pieces.at[there],
            received.at[seg],
            f_send.at[d],
            f_recv.at[d],
            device_id=(there, place),
            device_id_type=MESH,
        )

    for d in range(1, SEGS):
        piece_copy(d).start()
    mine = pltpu.make_async_copy(pieces.at[seg], received.at[seg], local_sem.at[0])

    @pl.when(folded)
    def _():
        piece_copy(0).start()

    @pl.when(jnp.logical_not(folded))
    def _():
        mine.start()

    def sent(half):
        for n in (1, 2, 3):
            own_copy(half, n).wait_send()

    sent(1)

    @pl.when(seg >= EARLY)
    def _():
        sent(0)

    @pl.when(seg < EARLY)
    def _():
        for n in range(1, SEGS):
            for k in range(2 if chips > 1 else 1):
                cut_copy(n, k).wait_send()

    def early_sent(number, carry):
        @pl.when(seg != number)
        def _():
            for n in peers:
                spread_copy(number, n).wait_send()
            cross_copy(number, plane).wait_send()

        return carry

    def late_sent(number, carry):
        same = lax.rem(source(number), 2) == column

        @pl.when(same)
        def _():
            facing_copy(number).wait_send()

        @pl.when(jnp.logical_not(same))
        def _():
            cross_copy(number, 1 - plane).wait_send()

        return carry

    lax.fori_loop(0, EARLY, early_sent, 0)
    lax.fori_loop(EARLY, SECTIONS, late_sent, 0)

    @pl.when(folded)
    def _():
        swap_copy.wait_send()

    def finish(number, carry):
        @pl.when((number < SECTIONS) & (source(number) != seg))
        def _():
            sibling_copy(number, core).wait_send()

        for way in range(2):
            halo_copy(number, way).wait_send()
        return carry

    lax.fori_loop(0, SECTIONS + 1, finish, 0)
    for d in range(1, SEGS):
        piece_copy(d).wait()

    @pl.when(folded)
    def _():
        piece_copy(0).wait()

    @pl.when(jnp.logical_not(folded))
    def _():
        mine.wait()

    for m in range(4):
        at = jnp.int32(0)
        for t in range(1, 4):
            at = jnp.where(order_ref[t] == m, 4 * (t // 2) + t % 2, at)
        for a in range(2):
            piece = received[at + 2 * a].astype(F32)
            for g in range(3):
                turned = pltpu.roll(piece, 128 - 32 * g, 1) if g else piece
                out_ref[m, a, ROWS * g : ROWS * g + ROWS] = turned.astype(BF)


def split3(x):
    high = x.astype(BF).astype(F32)
    middle = (x - high).astype(BF).astype(F32)
    return high, middle, x - high - middle


def per_device(
    fields, entry_order, shift_offsets, qkv_weight, out_weight, up_weight, down_weight,
    attn_bias, norm_gain,
):
    dma = pltpu.SemaphoreType.DMA
    stored = (
        fields.transpose(0, 2, 3, 1, 4), qkv_weight[:, 0], out_weight[:, 0], up_weight[:, 0],
        down_weight[:, 0].swapaxes(1, 2), attn_bias[:, 0],
    )
    vmem = pl.BlockSpec(memory_space=pltpu.VMEM)
    smem = pl.BlockSpec(memory_space=pltpu.SMEM)
    got = pl.pallas_call(
        kernel,
        out_shape=jax.ShapeDtypeStruct((4, 2, TOK, 128), BF),
        in_specs=[smem, smem, vmem] + [pl.BlockSpec(memory_space=pl.ANY)] * 6,
        out_specs=vmem,
        scratch_shapes=[pltpu.VMEM(a.shape, a.dtype) for a in stored] + [
            pltpu.VMEM((SECTIONS, PACK, 128), BF),
            pltpu.VMEM((2, PACK, 128), BF),
            pltpu.VMEM((SECTIONS + 1, 3 * TOK, 256), BF),
            pltpu.VMEM((TOK, 128), F32),
            pltpu.VMEM((TOK, 128), F32),
            pltpu.VMEM((768, 1024), BF),
            pltpu.VMEM((TOK, 256), F32),
            pltpu.VMEM((TOK, 256), BF),
            pltpu.VMEM((8, 256), F32),
            pltpu.VMEM((SEGS, ROWS, 128), BF),
            pltpu.VMEM((SEGS, ROWS, 128), BF),
            dma((1,)), dma((2,)), dma((SEGS, 2)), dma((EARLY,)), dma((EARLY, 8)), dma((EARLY,)),
            dma((SECTIONS,)), dma((SECTIONS,)), dma((SECTIONS,)), dma((SECTIONS,)), dma((2, 4)),
            dma((SECTIONS,)), dma((SECTIONS,)), dma((SECTIONS,)), dma((SECTIONS + 1, 2)), dma((SECTIONS + 1, 2)), dma((SEGS,)),
            dma((SEGS,)), dma((6, 2)),
        ],
        compiler_params=pltpu.CompilerParams(
            collective_id=0, has_side_effects=True, vmem_limit_bytes=56 * 2**20
        ),
        name="sections",
    )(entry_order, shift_offsets.transpose(1, 2, 0), norm_gain[:, 0], *stored)
    share = WIDTH // SEGS
    got = got[..., :share].reshape(4, 12, LON, 2, share)
    return got.transpose(0, 3, 1, 2, 4)


def solution(mesh):
    placed = (
        P(None, None, None, "lon", None),
        P(),
        P(None, None, "segment"),
        P(None, "segment", None, None),
        P(None, "segment", None, None),
        P(None, "segment", None, None),
        P(None, "segment", None, None),
        P(None, "segment", None, None, None, None),
        P(None, "segment", None, None),
    )
    return jax.shard_map(
        per_device,
        mesh=mesh,
        in_specs=placed,
        out_specs=P(None, None, None, "lon", "segment"),
        check_vma=False,
    )
```

```python
import functools
import math

import jax
import jax.numpy as jnp
from jax import lax
from jax.experimental import pallas as pl
from jax.experimental.pallas import tpu as pltpu
from jax.sharding import PartitionSpec as P

BF = jnp.bfloat16
F32 = jnp.float32
MESH = pl.DeviceIdType.MESH
NT = (((1,), (1,)), ((), ()))
TN = (((0,), (0,)), ((), ()))
NN = (((1,), (0,)), ((), ()))

SEGS = 8
SECTIONS = 16
EARLY = 4
HEADS = 6
TOK = 144
WIDTH = 192
LON = 12
STRIP = 192
BIAS = 6 * STRIP
PARAMS = BIAS + 7 * TOK
AFTER = BIAS + 8 * TOK
PACK = AFTER + 12 * STRIP
HALF = PACK // 2
CHUNKS = ((0, 2560), (2560, 2048))
ROWS = TOK // 3
FOLD = TOK // 2
BAND = TOK + FOLD + 8
EPS = 1e-5
QSCALE = math.log2(math.e) / math.sqrt(32.0)


def dot(a, b, dims=NN):
    return lax.dot_general(a, b, dims, preferred_element_type=F32)


def side(parts):
    return jnp.concatenate(parts, axis=1)


def down(parts):
    return jnp.concatenate(parts, axis=0)


def lanes(shape):
    return lax.broadcasted_iota(jnp.int32, shape, len(shape) - 1)


def normalize(x, gain, inside):
    mean = jnp.sum(x, axis=-1, keepdims=True) * (1.0 / WIDTH)
    centred = x - mean * inside
    spread = jnp.sum(centred * centred, axis=-1, keepdims=True) * (1.0 / WIDTH)
    return (centred * lax.rsqrt(spread + EPS) * gain).astype(BF)


def pick(token, lon, shift):
    x = lon + shift
    west, east = x < 0, x > LON - 1
    block = jnp.where(west, 0.0, jnp.where(east, 2.0, 1.0))
    of = token + shift + jnp.where(west, float(LON), jnp.where(east, float(-LON), 0.0))
    upper = of >= FOLD
    first = block * float(TOK) + of
    second = block * float(BAND - TOK) + jnp.where(upper, of - float(FOLD), of)
    col = lanes((TOK, 128)).astype(F32)

    def hot(hit):
        return jnp.where(hit, 1.0, 0.0).astype(BF)

    take = side([hot(col + float(128 * j) == first) for j in range(4)])[:, : 3 * TOK]
    hits = [col + float(128 * j) == second for j in range(2)]
    rest = down(
        [side([hot(hit & half) for hit in hits]) for half in (jnp.logical_not(upper), upper)]
    )[:, : 3 * (BAND - TOK)]
    return take, rest


def taken(chosen, bands, at):
    take, rest = chosen
    starts = (0, BAND, 2 * BAND)
    first = dot(take, down([bands[at, r : r + TOK, :] for r in starts]))
    second = dot(rest, down([bands[at, r + TOK : r + BAND, :] for r in starts]))
    low = jnp.where(lanes((1, 128)) < 64, 1.0, 0.0)
    second = (second[:TOK] + pltpu.roll(second[TOK:], 64, 1)) * low
    return side([first, second])


def folded_band(h):
    rest = h[:FOLD, 128:] + pltpu.roll(h[FOLD:, 128:], 64, 1)
    return down([h[:, :128], rest, jnp.zeros((8, 128), F32)]).astype(BF)


def section(u, strip, bias, gain_a, gain_b, ready=None):
    col = lanes((1, 256))
    inside = jnp.where(col < WIDTH, 1.0, 0.0)
    low = jnp.where(lanes((1, 128)) < 64, 1.0, 0.0)
    normed = normalize(u, gain_a, inside)
    short = normed[:, :WIDTH]
    qk = dot(short, side([strip(0), strip(1), strip(2)]))
    qb = (qk[:, :256] * QSCALE).astype(BF)
    kb = side([qk[:, 256:], pltpu.roll(qk[:, 128:256], 64, 1)]).astype(BF)
    mixed = strip(4)
    vt = dot(side([strip(3), mixed]), normed, NT).astype(BF)
    zero = jnp.zeros((TOK, 256), BF)
    pos = lanes((TOK, 256))
    spread_q = down(
        [jnp.where((pos >= 32 * h) & (pos < 32 * h + 32), qb, zero) for h in range(HEADS)]
        + [jnp.zeros((32, 256), BF)]
    )
    scores = dot(kb, spread_q, NT) + side([bias(j) for j in range(7)]).astype(F32)
    top = jnp.max(scores, axis=0, keepdims=True)
    expo = jnp.exp2(scores - top)
    inverse = 1.0 / jnp.sum(expo, axis=0, keepdims=True)
    expo = expo.astype(BF)
    parts = []
    for h in range(HEADS):
        cut = slice(128 * h, 128 * h + 256)
        part = dot(vt[32 * h : 32 * h + 32], expo[:, cut]) * inverse[:, cut]
        if h:
            part = pltpu.roll(part, 256 - 16 * h, 1)
        parts.append(part[:, :TOK])
    context = down(parts).astype(BF)
    out = dot(context, side([strip(5), mixed]), TN)
    out = side([out[:, :128], pltpu.roll(out[:, 128:], 64, 1) * low])
    x1 = u + out.astype(BF).astype(F32)
    normed = normalize(x1, gain_b, inside)[:, :WIDTH]
    if ready is not None:
        ready()
    hidden = jax.nn.gelu(dot(normed, side([strip(6 + j) for j in range(6)]))).astype(BF)
    low_t = down([side([strip(12 + j) for j in range(6)]), jnp.zeros((64, 768), BF)])
    y = dot(hidden, low_t, NT)
    return x1 + y


def kernel(
    order_ref, shift_ref, gain_ref, *refs,
):
    given, out_ref, held, rest = refs[:6], refs[6], refs[7:13], refs[13:]
    fields_ref, qkv_ref, out_w_ref, up_ref, low_ref, bias_ref = held
    (
        packs, other, hist, token_ref, lon_ref, share_ref, stage, swap, gains, pieces, received,
        local_sem, swap_sem, a_send, a_recv, b_send, b_recv, e_send, e_recv, d_send,
        d_recv, x_send, x_recv,
        c_send, c_recv, w_send, w_recv, s_send, s_recv, h_send, h_recv, f_send, f_recv,
        in_sem,
    ) = rest
    seg = lax.axis_index("segment")
    me = lax.axis_index("lon")
    ring = lax.axis_size("lon")
    half_ring = ring // 2
    core = lax.rem(me, 2)
    sibling = me + 1 - 2 * core
    column = lax.rem(seg, 2)
    facing = seg + 1 - 2 * column
    slot = column + 2 * (seg // 4)
    lat = lax.rem(seg // 2, 2)
    across = lax.rem(me + half_ring, ring)
    folded = me >= half_ring

    def along(place):
        place = lax.rem(place + ring, ring)
        return jnp.where(place < half_ring, place, 3 * half_ring - 1 - place)

    place = along(me)
    west, east = along(place - 1), along(place + 1)

    def arrival(n, half):
        if n == 0:
            return pltpu.make_async_copy(given[0], held[0], in_sem.at[n, half])
        return pltpu.make_async_copy(given[n].at[half], held[n].at[half], in_sem.at[n, half])

    barrier = pltpu.get_barrier_semaphore()

    def greet(seg_to, lon_to):
        pl.semaphore_signal(barrier, inc=1, device_id=(seg_to, lon_to), device_id_type=MESH)

    for d in (2, 4, 6):
        greet(lax.rem(seg + d, SEGS), me)
    greet(facing, across)
    greet(seg, west)
    greet(seg, east)
    for d in range(1, SEGS):
        greet(lax.rem(seg + d, SEGS), place)
    greet(seg, jnp.where(folded, place, sibling))
    chips = half_ring // 2
    chip = lax.rem(me, half_ring) // 2
    plane = me // half_ring

    def on_chip(n):
        return plane * half_ring + 2 * lax.rem(chip + n, chips) + core

    for n in range(1, chips):
        greet(seg, on_chip(n))
    greet(seg, across)
    for n in range(1, 4):
        greet(lax.rem(facing + 2 * n, SEGS), across)

    for n in (5, 1, 2, 3, 4, 0):
        arrival(n, 0).start()
    for n in range(1, 6):
        arrival(n, 1).start()

    def source(number):
        return jnp.minimum(number, SECTIONS - 1 - number)

    def own_number(half):
        return seg if half == 0 else SECTIONS - 1 - seg

    def prepare(half):
        number = own_number(half)
        for n in range(1, 6):
            arrival(n, half).wait()

        def put(start, block):
            block = block.astype(BF)
            packs[number, start : start + block.shape[0], :] = block
            other[half, start : start + block.shape[0], :] = block

        def put_strip(j, block):
            put(STRIP * j if j < 6 else AFTER + STRIP * (j - 6), block)

        low = lanes((STRIP, 128)) < 64
        qkv = [qkv_ref[half, :, 128 * j : 128 * j + 128].astype(F32) for j in range(4)]
        put_strip(0, qkv[0])
        put_strip(1, jnp.where(low, qkv[1], qkv[2]))
        put_strip(2, jnp.where(low, pltpu.roll(qkv[1], 64, 1), pltpu.roll(qkv[2], 64, 1)))
        eye = (lax.broadcasted_iota(jnp.int32, (WIDTH, WIDTH), 0) == lanes((WIDTH, WIDTH)))
        turned = dot(jnp.where(eye, 1.0, 0.0).astype(BF), qkv_ref[half, :, 384:576], NT)
        out_w = out_w_ref[half].astype(F32)
        put_strip(3, turned[:, :128])
        put_strip(4, side([turned[:, 128:], out_w[:, 128:]]))
        put_strip(5, out_w[:, :128])
        for j in range(6):
            put_strip(6 + j, up_ref[half, :, 128 * j : 128 * j + 128])
            put_strip(12 + j, low_ref[half, :, 128 * j : 128 * j + 128])

        eye = (lax.broadcasted_iota(jnp.int32, (TOK, TOK), 0) == lanes((TOK, TOK)))
        eye = jnp.where(eye, 1.0, 0.0).astype(BF)

        def put_bias(window, store):
            table = bias_ref[half, window].reshape(HEADS * TOK, TOK)
            top = jnp.max(table, axis=-1, keepdims=True)
            table = ((table - top) * math.log2(math.e)).astype(BF)
            table = dot(eye, down([table, jnp.zeros((32, TOK), BF)]), NT).astype(BF)
            for j in range(7):
                store(BIAS + TOK * j, table[:, 128 * j : 128 * j + 128])

        def store_own(start, block):
            packs[number, start : start + TOK, :] = block

        def store_other(start, block):
            other[half, start : start + TOK, :] = block

        put_bias(lat, store_own)
        put_bias(1 - lat, store_other)
        gains[...] = jnp.zeros_like(gains)
        gains[0:2, :WIDTH] = gain_ref[half]
        rows = []
        for n in range(2):
            for part in split3(gains[n : n + 1, :]):
                rows += [part[:, :128], part[:, 128:]]
        rows += [jnp.full((1, 128), shift_ref[half, 0, t].astype(F32)) for t in range(4)]
        put(PARAMS, down(rows))
        rest = jnp.zeros((TOK - 16, 128), BF)
        put(PARAMS + 16, rest)

    half_rows = pl.ds(pl.multiple_of(core * HALF, 16), HALF)

    def part_rows(plane_of):
        start = core * HALF + plane_of * (HALF // 2)
        return pl.ds(pl.multiple_of(start, 16), HALF // 2)

    def own_copy(half, n):
        number = own_number(half)
        ref = packs.at[number] if n == 2 else other.at[half]
        return pltpu.make_async_remote_copy(
            ref.at[half_rows], packs.at[number, half_rows], w_send.at[half, n], w_recv.at[number],
            device_id=(lax.rem(seg + 2 * n, SEGS), me), device_id_type=MESH,
        )

    def send_weights(half):
        facing_copy(own_number(half)).start()
        for n in (1, 3, 2):
            own_copy(half, n).start()

    def facing_copy(number):
        rows = part_rows(plane)
        return pltpu.make_async_remote_copy(
            packs.at[number, rows], packs.at[number, rows], c_send.at[number], c_recv.at[number],
            device_id=(facing, across), device_id_type=MESH,
        )

    def cross_copy(number, plane_of):
        rows = part_rows(plane_of)
        return pltpu.make_async_remote_copy(
            packs.at[number, rows], packs.at[number, rows], x_send.at[number], x_recv.at[number],
            device_id=(seg, across), device_id_type=MESH,
        )

    def sibling_copy(number, start):
        start = pl.multiple_of(start * HALF, 16)
        return pltpu.make_async_remote_copy(
            packs.at[number, pl.ds(start, HALF)],
            packs.at[number, pl.ds(start, HALF)],
            s_send.at[number],
            s_recv.at[number],
            device_id=(seg, sibling),
            device_id_type=MESH,
        )

    def first(number):
        seg_of = source(number)

        @pl.when((seg_of != seg) & (lax.rem(seg_of, 2) == column))
        def _():
            pltpu.make_async_remote_copy(
                packs.at[number, half_rows], packs.at[number, half_rows], w_send.at[0, 0],
                w_recv.at[number], device_id=(facing, across), device_id_type=MESH,
            ).wait_recv()
            facing_copy(number).start()
            sibling_copy(number, core).start()

    def second(number):
        @pl.when(lax.rem(source(number), 2) != column)
        def _():
            rows = part_rows(1 - plane)
            pltpu.make_async_remote_copy(
                packs.at[number, rows], packs.at[number, rows], c_send.at[number],
                c_recv.at[number], device_id=(facing, across), device_id_type=MESH,
            ).wait_recv()
            cross_copy(number, 1 - plane).start()

    def third(number):
        @pl.when(lax.rem(source(number), 2) != column)
        def _():
            cross_copy(number, plane).wait_recv()
            sibling_copy(number, core).start()

    far = max(1, chips // 2)
    pair = min(2, chips)
    at_z = lax.rem(chip, far) * pair + chip // far

    def core_rows(core_of, k):
        start, size = CHUNKS[k]
        return pl.ds(pl.multiple_of(start + core_of * (size // 2), 16), size // 2)

    def plane_rows(plane_of, k):
        start, size = CHUNKS[k]
        start = start + core * (size // 2) + plane_of * (size // 4)
        return pl.ds(pl.multiple_of(start, 16), size // 4)

    def cut_rows(plane_of, k, first_cut, count):
        start, size = CHUNKS[k]
        cut = size // 4 // chips
        start = start + core * (size // 2) + plane_of * (size // 4) + first_cut * cut
        return pl.ds(pl.multiple_of(start, 16), count * cut)

    def pair_rows(plane_of, k):
        return cut_rows(plane_of, k, lax.rem(chip, far) * pair, pair)

    def early_copy(number, rows, send, recv, seg_to, lon_to, ref=None):
        ref = packs.at[number] if ref is None else ref
        return pltpu.make_async_remote_copy(
            ref.at[rows], packs.at[number, rows], send, recv,
            device_id=(seg_to, lon_to), device_id_type=MESH,
        )

    def cut_copy(n, k):
        if n < 4:
            seg_to, lon_to, rows = seg + 2 * n, me, pair_rows(plane, k)
        else:
            seg_to, lon_to, rows = facing + 2 * n, across, pair_rows(1 - plane, k)
        recv = a_recv.at[2 * jnp.minimum(seg, EARLY - 1) + k]
        ref = other.at[0] if n % 2 else packs.at[seg]
        return early_copy(seg, rows, a_send.at[n, k], recv, lax.rem(seg_to, SEGS), lon_to, ref)

    def send_cuts():
        for k in range(2):
            for n in (4, 1, 3, 5, 7, 2, 6):
                cut_copy(n, k).start()

    peers = [n for m in range(1, chips // 2) for n in (m, chips - m)]

    def spread_copy(number, k, n):
        at = 2 * number + k
        rows = cut_rows(plane, k, at_z, 1)
        return early_copy(number, rows, b_send.at[at, n], b_recv.at[at], seg, on_chip(n))

    def spread(number, k):
        @pl.when(seg != number)
        def _():
            at = 2 * number + k
            rows = pair_rows(plane, k)
            early_copy(number, rows, a_send.at[0, 0], a_recv.at[at], seg, across).wait_recv()
            for n in peers:
                spread_copy(number, k, n).start()

    def plane_copy(number, k, plane_of):
        at = 2 * number + k
        rows = plane_rows(plane_of, k)
        return early_copy(number, rows, e_send.at[at], e_recv.at[at], seg, across)

    def cross(number, k):
        @pl.when(seg != number)
        def _():
            if peers:
                at = 2 * number + k
                rows = cut_rows(plane, k, 0, len(peers))
                early_copy(number, rows, a_send.at[0, 0], b_recv.at[at], seg, across).wait_recv()
            plane_copy(number, k, plane).start()

    def core_copy(number, k, core_of):
        at = 2 * number + k
        rows = core_rows(core_of, k)
        return early_copy(number, rows, d_send.at[at], d_recv.at[at], seg, sibling)

    def pair_up(number, k):
        @pl.when(seg != number)
        def _():
            plane_copy(number, k, 1 - plane).wait_recv()
            core_copy(number, k, core).start()

    def halo_copy(number, way):
        return pltpu.make_async_remote_copy(
            hist.at[number, pl.ds(BAND, BAND)],
            hist.at[number, pl.ds(2 * BAND if way == 0 else 0, BAND)],
            h_send.at[number, way],
            h_recv.at[number, way],
            device_id=(seg, west if way == 0 else east),
            device_id_type=MESH,
        )

    swap_copy = pltpu.make_async_remote_copy(
        swap, hist.at[0, pl.ds(BAND, BAND)], swap_sem.at[0], swap_sem.at[1],
        device_id=(seg, place), device_id_type=MESH,
    )

    prepare(0)
    stage[...] = jnp.zeros_like(stage)
    arrival(0, 0).wait()
    micro = order_ref[slot]
    for n in range(6):
        cells = fields_ref[micro, 6 * lat + n].astype(F32)
        for level in range(2):
            start = 72 * level + LON * n
            stage[start : start + LON, :WIDTH] = cells[:, level, :]

    pl.semaphore_wait(barrier, 14 + chips + 3)

    @pl.when(seg < EARLY)
    def _():
        send_cuts()

    @pl.when(seg >= EARLY)
    def _():
        send_weights(0)


    @pl.when(folded)
    def _():
        swap[...] = folded_band(stage[...])
        swap_copy.start()
        swap_copy.wait_recv()

    @pl.when(jnp.logical_not(folded))
    def _():
        hist[0, BAND : 2 * BAND] = folded_band(stage[...])

    for way in range(2):
        halo_copy(0, way).start()
    token = lax.broadcasted_iota(jnp.int32, (TOK, 128), 0)
    token_ref[...] = token.astype(F32)
    share = WIDTH // SEGS
    feature = lax.broadcasted_iota(jnp.int32, (256, 128), 0)
    for g in range(3):
        lane = lanes((256, 128)) - 32 * g
        inside = (lane >= 0) & (lane < share)
        for s in range(SEGS):
            hit = inside & (feature == lane + share * s)
            share_ref[256 * g : 256 * g + 256, 128 * s : 128 * s + 128] = jnp.where(
                hit, 1.0, 0.0
            ).astype(BF)
    lon_ref[...] = lax.rem(token, LON).astype(F32)
    spread(0, 0)
    spread(0, 1)
    cross(0, 0)
    spread(1, 0)
    cross(0, 1)
    spread(1, 1)
    pair_up(0, 0)
    cross(1, 0)
    pair_up(0, 1)
    spread(2, 0)
    prepare(1)
    cross(1, 1)
    spread(2, 1)

    def params(number):
        return packs[number, PARAMS : PARAMS + 16, :].astype(F32)

    def offset(tile):
        row = lax.broadcasted_iota(jnp.int32, (16, 128), 0)
        return jnp.sum(jnp.where(row == 12 + slot, tile, 0.0), axis=0, keepdims=True)

    def step(number, decoder):
        if not decoder:
            @pl.when(number == 0)
            def _():
                @pl.when((seg >= 0) & (seg < 8))
                def _():
                    send_weights(1)

            @pl.when(number == 1)
            def _():
                pair_up(1, 0)
                pair_up(1, 1)
                cross(2, 0)
                cross(2, 1)
                spread(3, 0)
                spread(3, 1)

            @pl.when(number == 2)
            def _():
                pair_up(2, 0)
                pair_up(2, 1)
                cross(3, 0)
                cross(3, 1)
                first(4)
                first(5)

            @pl.when(number == 3)
            def _():
                pair_up(3, 0)
                pair_up(3, 1)
                second(4)
                second(5)
                first(6)
                first(7)

            @pl.when(number == 4)
            def _():
                third(4)
                second(6)

            @pl.when(number == 5)
            def _():
                third(5)
                second(7)

            @pl.when(number == 6)
            def _():
                third(6)
                third(7)

        @pl.when((number >= 7) & (number < SECTIONS - 1))
        def _():
            third(number + 1)

        @pl.when((number >= 6) & (number < SECTIONS - 2))
        def _():
            second(number + 2)

        @pl.when((number >= 4) & (number < SECTIONS - 4))
        def _():
            first(number + 4)

        def early(k):
            for n in range(EARLY):
                @pl.when((number == n) & (seg != n))
                def _():
                    core_copy(n, k, 1 - core).wait_recv()

        @pl.when((source(number) != seg) & (number >= EARLY))
        def _():
            sibling_copy(number, 1 - core).wait_recv()

        if not decoder:
            early(0)

        tile = params(number)
        now = offset(tile)
        if decoder:
            before = offset(params(number - 1))
            earlier = now - offset(params(15 - number))
            aside = taken(pick(token_ref[...], lon_ref[...], earlier), hist, 16 - number)
        else:
            before = offset(params(jnp.maximum(number - 1, 0)))
            before = before * jnp.where(number > 0, 1.0, 0.0)
        chosen = pick(token_ref[...], lon_ref[...], now - before)
        for way in range(2):
            halo_copy(number, way).wait_recv()
        u = taken(chosen, hist, number)
        if decoder:
            u = ((u + aside) * 0.5).astype(BF).astype(F32)
        gain_a = side([tile[0:1] + tile[2:3] + tile[4:5], tile[1:2] + tile[3:4] + tile[5:6]])
        gain_b = side([tile[6:7] + tile[8:9] + tile[10:11], tile[7:8] + tile[9:10] + tile[11:12]])

        def strip(j):
            start = STRIP * j if j < 6 else AFTER + STRIP * (j - 6)
            return packs[number, start : start + STRIP, :]

        def bias(j):
            return packs[number, BIAS + TOK * j : BIAS + TOK * j + TOK, :]

        made = section(
            u, strip, bias, gain_a, gain_b, None if decoder else functools.partial(early, 1)
        )
        hist[number + 1, BAND : 2 * BAND] = folded_band(made)
        for way in range(2):
            halo_copy(number + 1, way).start()

    lax.fori_loop(0, 9, lambda i, c: (step(i, False), c)[1], 0)
    lax.fori_loop(9, SECTIONS, lambda i, c: (step(i, True), c)[1], 0)

    order = lax.broadcasted_iota(jnp.int32, (TOK, 128), 0)
    lon = lax.rem(order, 24) // 2
    token = (lax.rem(order, 2) * 6 + order // 24) * LON + lon
    back = pick(token.astype(F32), lon.astype(F32), -offset(params(SECTIONS - 1)))
    for way in range(2):
        halo_copy(SECTIONS, way).wait_recv()
    final = taken(back, hist, SECTIONS).astype(BF)
    final = side([final[ROWS * g : ROWS * g + ROWS] for g in range(3)])
    final = dot(final, share_ref[...]).astype(BF)
    for s in range(SEGS):
        pieces[s] = final[:, 128 * s : 128 * s + 128]

    def piece_copy(d):
        there = lax.rem(seg + d, SEGS)
        return pltpu.make_async_remote_copy(
            pieces.at[there],
            received.at[seg],
            f_send.at[d],
            f_recv.at[d],
            device_id=(there, place),
            device_id_type=MESH,
        )

    for d in range(1, SEGS):
        piece_copy(d).start()
    mine = pltpu.make_async_copy(pieces.at[seg], received.at[seg], local_sem.at[0])

    @pl.when(folded)
    def _():
        piece_copy(0).start()

    @pl.when(jnp.logical_not(folded))
    def _():
        mine.start()

    def sent(half):
        for n in (1, 2, 3):
            own_copy(half, n).wait_send()

    sent(1)

    @pl.when(seg >= EARLY)
    def _():
        sent(0)

    @pl.when(seg < EARLY)
    def _():
        for k in range(2):
            for n in range(1, SEGS):
                cut_copy(n, k).wait_send()

    def early_sent(number, carry):
        @pl.when(seg != number)
        def _():
            for k in range(2):
                for n in peers:
                    spread_copy(number, k, n).wait_send()
                plane_copy(number, k, plane).wait_send()
                core_copy(number, k, core).wait_send()

        return carry

    def late_sent(number, carry):
        same = lax.rem(source(number), 2) == column

        @pl.when(same)
        def _():
            facing_copy(number).wait_send()

        @pl.when(jnp.logical_not(same))
        def _():
            cross_copy(number, 1 - plane).wait_send()

        return carry

    lax.fori_loop(0, EARLY, early_sent, 0)
    lax.fori_loop(EARLY, SECTIONS, late_sent, 0)

    @pl.when(folded)
    def _():
        swap_copy.wait_send()

    def finish(number, carry):
        @pl.when((number >= EARLY) & (number < SECTIONS) & (source(number) != seg))
        def _():
            sibling_copy(number, core).wait_send()

        for way in range(2):
            halo_copy(number, way).wait_send()
        return carry

    lax.fori_loop(0, SECTIONS + 1, finish, 0)
    for d in range(1, SEGS):
        piece_copy(d).wait()

    @pl.when(folded)
    def _():
        piece_copy(0).wait()

    @pl.when(jnp.logical_not(folded))
    def _():
        mine.wait()

    for m in range(4):
        at = jnp.int32(0)
        for t in range(1, 4):
            at = jnp.where(order_ref[t] == m, 4 * (t // 2) + t % 2, at)
        for a in range(2):
            piece = received[at + 2 * a].astype(F32)
            for g in range(3):
                turned = pltpu.roll(piece, 128 - 32 * g, 1) if g else piece
                out_ref[m, a, ROWS * g : ROWS * g + ROWS] = turned.astype(BF)


def split3(x):
    high = x.astype(BF).astype(F32)
    middle = (x - high).astype(BF).astype(F32)
    return high, middle, x - high - middle


def per_device(
    fields, entry_order, shift_offsets, qkv_weight, out_weight, up_weight, down_weight,
    attn_bias, norm_gain,
):
    dma = pltpu.SemaphoreType.DMA
    stored = (
        fields.transpose(0, 2, 3, 1, 4), qkv_weight[:, 0], out_weight[:, 0], up_weight[:, 0],
        down_weight[:, 0].swapaxes(1, 2), attn_bias[:, 0],
    )
    vmem = pl.BlockSpec(memory_space=pltpu.VMEM)
    smem = pl.BlockSpec(memory_space=pltpu.SMEM)
    got = pl.pallas_call(
        kernel,
        out_shape=jax.ShapeDtypeStruct((4, 2, TOK, 128), BF),
        in_specs=[smem, smem, vmem] + [pl.BlockSpec(memory_space=pl.ANY)] * 6,
        out_specs=vmem,
        scratch_shapes=[pltpu.VMEM(a.shape, a.dtype) for a in stored] + [
            pltpu.VMEM((SECTIONS, PACK, 128), BF),
            pltpu.VMEM((2, PACK, 128), BF),
            pltpu.VMEM((SECTIONS + 1, 3 * BAND, 128), BF),
            pltpu.VMEM((TOK, 128), F32),
            pltpu.VMEM((TOK, 128), F32),
            pltpu.VMEM((768, 1024), BF),
            pltpu.VMEM((TOK, 256), F32),
            pltpu.VMEM((BAND, 128), BF),
            pltpu.VMEM((8, 256), F32),
            pltpu.VMEM((SEGS, ROWS, 128), BF),
            pltpu.VMEM((SEGS, ROWS, 128), BF),
            dma((1,)), dma((2,)), dma((SEGS, 2)), dma((2 * EARLY,)), dma((2 * EARLY, 8)),
            dma((2 * EARLY,)), dma((2 * EARLY,)), dma((2 * EARLY,)), dma((2 * EARLY,)),
            dma((2 * EARLY,)),
            dma((SECTIONS,)), dma((SECTIONS,)), dma((SECTIONS,)), dma((SECTIONS,)), dma((2, 4)),
            dma((SECTIONS,)), dma((SECTIONS,)), dma((SECTIONS,)), dma((SECTIONS + 1, 2)), dma((SECTIONS + 1, 2)), dma((SEGS,)),
            dma((SEGS,)), dma((6, 2)),
        ],
        compiler_params=pltpu.CompilerParams(
            collective_id=0, has_side_effects=True, vmem_limit_bytes=56 * 2**20
        ),
        name="sections",
    )(entry_order, shift_offsets.transpose(1, 2, 0), norm_gain[:, 0], *stored)
    share = WIDTH // SEGS
    got = got[..., :share].reshape(4, 12, LON, 2, share)
    return got.transpose(0, 3, 1, 2, 4)


def solution(mesh):
    placed = (
        P(None, None, None, "lon", None),
        P(),
        P(None, None, "segment"),
        P(None, "segment", None, None),
        P(None, "segment", None, None),
        P(None, "segment", None, None),
        P(None, "segment", None, None),
        P(None, "segment", None, None, None, None),
        P(None, "segment", None, None),
    )
    return jax.shard_map(
        per_device,
        mesh=mesh,
        in_specs=placed,
        out_specs=P(None, None, None, "lon", "segment"),
        check_vma=False,
    )
```

```python
import functools
import math

import jax
import jax.numpy as jnp
from jax import lax
from jax.experimental import pallas as pl
from jax.experimental.pallas import tpu as pltpu
from jax.sharding import PartitionSpec as P

BF = jnp.bfloat16
F32 = jnp.float32
MESH = pl.DeviceIdType.MESH
NT = (((1,), (1,)), ((), ()))
TN = (((0,), (0,)), ((), ()))
NN = (((1,), (0,)), ((), ()))

SEGS = 8
SECTIONS = 16
EARLY = 4
HEADS = 6
TOK = 144
WIDTH = 192
LON = 12
STRIP = 192
BIAS = 6 * STRIP
PARAMS = BIAS + 7 * TOK
AFTER = BIAS + 8 * TOK
PACK = AFTER + 12 * STRIP
HALF = PACK // 2
CHUNKS = ((0, 2560), (2560, 2048))
ROWS = TOK // 3
FOLD = TOK // 2
BAND = TOK + FOLD + 8
EPS = 1e-5
QSCALE = math.log2(math.e) / math.sqrt(32.0)


def dot(a, b, dims=NN):
    return lax.dot_general(a, b, dims, preferred_element_type=F32)


def side(parts):
    return jnp.concatenate(parts, axis=1)


def down(parts):
    return jnp.concatenate(parts, axis=0)


def lanes(shape):
    return lax.broadcasted_iota(jnp.int32, shape, len(shape) - 1)


def normalize(x, gain, inside):
    mean = jnp.sum(x, axis=-1, keepdims=True) * (1.0 / WIDTH)
    centred = x - mean * inside
    spread = jnp.sum(centred * centred, axis=-1, keepdims=True) * (1.0 / WIDTH)
    return (centred * lax.rsqrt(spread + EPS) * gain).astype(BF)


def pick(token, lon, shift):
    x = lon + shift
    west, east = x < 0, x > LON - 1
    block = jnp.where(west, 0.0, jnp.where(east, 2.0, 1.0))
    of = token + shift + jnp.where(west, float(LON), jnp.where(east, float(-LON), 0.0))
    upper = of >= FOLD
    first = block * float(TOK) + of
    second = block * float(BAND - TOK) + jnp.where(upper, of - float(FOLD), of)
    col = lanes((TOK, 128)).astype(F32)

    def hot(hit):
        return jnp.where(hit, 1.0, 0.0).astype(BF)

    take = side([hot(col + float(128 * j) == first) for j in range(4)])[:, : 3 * TOK]
    hits = [col + float(128 * j) == second for j in range(2)]
    rest = down(
        [side([hot(hit & half) for hit in hits]) for half in (jnp.logical_not(upper), upper)]
    )[:, : 3 * (BAND - TOK)]
    return take, rest


def taken(chosen, bands, at):
    take, rest = chosen
    starts = (0, BAND, 2 * BAND)
    first = dot(take, down([bands[at, r : r + TOK, :] for r in starts]))
    second = dot(rest, down([bands[at, r + TOK : r + BAND, :] for r in starts]))
    low = jnp.where(lanes((1, 128)) < 64, 1.0, 0.0)
    second = (second[:TOK] + pltpu.roll(second[TOK:], 64, 1)) * low
    return side([first, second])


def folded_band(h):
    rest = h[:FOLD, 128:] + pltpu.roll(h[FOLD:, 128:], 64, 1)
    return down([h[:, :128], rest, jnp.zeros((8, 128), F32)]).astype(BF)


def section(u, strip, bias, gain_a, gain_b, ready=None):
    col = lanes((1, 256))
    inside = jnp.where(col < WIDTH, 1.0, 0.0)
    low = jnp.where(lanes((1, 128)) < 64, 1.0, 0.0)
    normed = normalize(u, gain_a, inside)
    short = normed[:, :WIDTH]
    qk = dot(short, side([strip(0), strip(1), strip(2)]))
    qb = (qk[:, :256] * QSCALE).astype(BF)
    kb = side([qk[:, 256:], pltpu.roll(qk[:, 128:256], 64, 1)]).astype(BF)
    mixed = strip(4)
    vt = dot(side([strip(3), mixed]), normed, NT).astype(BF)
    zero = jnp.zeros((TOK, 256), BF)
    pos = lanes((TOK, 256))
    spread_q = down(
        [jnp.where((pos >= 32 * h) & (pos < 32 * h + 32), qb, zero) for h in range(HEADS)]
        + [jnp.zeros((32, 256), BF)]
    )
    scores = dot(kb, spread_q, NT) + side([bias(j) for j in range(7)]).astype(F32)
    top = jnp.max(scores, axis=0, keepdims=True)
    expo = jnp.exp2(scores - top)
    inverse = 1.0 / jnp.sum(expo, axis=0, keepdims=True)
    expo = expo.astype(BF)
    parts = []
    for h in range(HEADS):
        cut = slice(128 * h, 128 * h + 256)
        part = dot(vt[32 * h : 32 * h + 32], expo[:, cut]) * inverse[:, cut]
        if h:
            part = pltpu.roll(part, 256 - 16 * h, 1)
        parts.append(part[:, :TOK])
    context = down(parts).astype(BF)
    out = dot(context, side([strip(5), mixed]), TN)
    out = side([out[:, :128], pltpu.roll(out[:, 128:], 64, 1) * low])
    x1 = u + out.astype(BF).astype(F32)
    normed = normalize(x1, gain_b, inside)[:, :WIDTH]
    if ready is not None:
        ready()
    hidden = jax.nn.gelu(dot(normed, side([strip(6 + j) for j in range(6)]))).astype(BF)
    low_t = down([side([strip(12 + j) for j in range(6)]), jnp.zeros((64, 768), BF)])
    y = dot(hidden, low_t, NT)
    return x1 + y


def kernel(
    order_ref, shift_ref, gain_ref, *refs,
):
    given, out_ref, held, rest = refs[:6], refs[6], refs[7:13], refs[13:]
    fields_ref, qkv_ref, out_w_ref, up_ref, low_ref, bias_ref = held
    (
        packs, other, hist, token_ref, lon_ref, share_ref, stage, swap, gains, pieces, received,
        local_sem, swap_sem, a_send, a_recv, b_send, b_recv, e_send, e_recv, d_send,
        d_recv, x_send, x_recv,
        c_send, c_recv, w_send, w_recv, s_send, s_recv, h_send, h_recv, f_send, f_recv,
        in_sem,
    ) = rest
    seg = lax.axis_index("segment")
    me = lax.axis_index("lon")
    ring = lax.axis_size("lon")
    half_ring = ring // 2
    core = lax.rem(me, 2)
    sibling = me + 1 - 2 * core
    column = lax.rem(seg, 2)
    facing = seg + 1 - 2 * column
    slot = column + 2 * (seg // 4)
    lat = lax.rem(seg // 2, 2)
    across = lax.rem(me + half_ring, ring)
    folded = me >= half_ring

    def along(place):
        place = lax.rem(place + ring, ring)
        return jnp.where(place < half_ring, place, 3 * half_ring - 1 - place)

    place = along(me)
    west, east = along(place - 1), along(place + 1)

    def arrival(n, half):
        if n == 0:
            return pltpu.make_async_copy(given[0], held[0], in_sem.at[n, half])
        return pltpu.make_async_copy(given[n].at[half], held[n].at[half], in_sem.at[n, half])

    barrier = pltpu.get_barrier_semaphore()

    def greet(seg_to, lon_to):
        pl.semaphore_signal(barrier, inc=1, device_id=(seg_to, lon_to), device_id_type=MESH)

    for d in (2, 4, 6):
        greet(lax.rem(seg + d, SEGS), me)
    greet(facing, across)
    greet(seg, west)
    greet(seg, east)
    for d in range(1, SEGS):
        greet(lax.rem(seg + d, SEGS), place)
    greet(seg, jnp.where(folded, place, sibling))
    chips = half_ring // 2
    chip = lax.rem(me, half_ring) // 2
    plane = me // half_ring

    def on_chip(n):
        return plane * half_ring + 2 * lax.rem(chip + n, chips) + core

    for n in range(1, chips):
        greet(seg, on_chip(n))
    greet(seg, across)
    for n in range(1, 4):
        greet(lax.rem(facing + 2 * n, SEGS), across)

    for n in (5, 1, 2, 3, 4, 0):
        arrival(n, 0).start()
    for n in range(1, 6):
        arrival(n, 1).start()

    def source(number):
        return jnp.minimum(number, SECTIONS - 1 - number)

    def own_number(half):
        return seg if half == 0 else SECTIONS - 1 - seg

    def prepare(half):
        number = own_number(half)
        for n in range(1, 6):
            arrival(n, half).wait()

        def put(start, block):
            block = block.astype(BF)
            packs[number, start : start + block.shape[0], :] = block
            other[half, start : start + block.shape[0], :] = block

        def put_strip(j, block):
            put(STRIP * j if j < 6 else AFTER + STRIP * (j - 6), block)

        low = lanes((STRIP, 128)) < 64
        qkv = [qkv_ref[half, :, 128 * j : 128 * j + 128].astype(F32) for j in range(4)]
        put_strip(0, qkv[0])
        put_strip(1, jnp.where(low, qkv[1], qkv[2]))
        put_strip(2, jnp.where(low, pltpu.roll(qkv[1], 64, 1), pltpu.roll(qkv[2], 64, 1)))
        eye = (lax.broadcasted_iota(jnp.int32, (WIDTH, WIDTH), 0) == lanes((WIDTH, WIDTH)))
        turned = dot(jnp.where(eye, 1.0, 0.0).astype(BF), qkv_ref[half, :, 384:576], NT)
        out_w = out_w_ref[half].astype(F32)
        put_strip(3, turned[:, :128])
        put_strip(4, side([turned[:, 128:], out_w[:, 128:]]))
        put_strip(5, out_w[:, :128])
        for j in range(6):
            put_strip(6 + j, up_ref[half, :, 128 * j : 128 * j + 128])
            put_strip(12 + j, low_ref[half, :, 128 * j : 128 * j + 128])

        eye = (lax.broadcasted_iota(jnp.int32, (TOK, TOK), 0) == lanes((TOK, TOK)))
        eye = jnp.where(eye, 1.0, 0.0).astype(BF)

        def put_bias(window, store):
            table = bias_ref[half, window].reshape(HEADS * TOK, TOK)
            top = jnp.max(table, axis=-1, keepdims=True)
            table = ((table - top) * math.log2(math.e)).astype(BF)
            table = dot(eye, down([table, jnp.zeros((32, TOK), BF)]), NT).astype(BF)
            for j in range(7):
                store(BIAS + TOK * j, table[:, 128 * j : 128 * j + 128])

        def store_own(start, block):
            packs[number, start : start + TOK, :] = block

        def store_other(start, block):
            other[half, start : start + TOK, :] = block

        put_bias(lat, store_own)
        put_bias(1 - lat, store_other)
        gains[...] = jnp.zeros_like(gains)
        gains[0:2, :WIDTH] = gain_ref[half]
        rows = []
        for n in range(2):
            for part in split3(gains[n : n + 1, :]):
                rows += [part[:, :128], part[:, 128:]]
        rows += [jnp.full((1, 128), shift_ref[half, 0, t].astype(F32)) for t in range(4)]
        put(PARAMS, down(rows))
        rest = jnp.zeros((TOK - 16, 128), BF)
        put(PARAMS + 16, rest)

    half_rows = pl.ds(pl.multiple_of(core * HALF, 16), HALF)

    def part_rows(plane_of):
        start = core * HALF + plane_of * (HALF // 2)
        return pl.ds(pl.multiple_of(start, 16), HALF // 2)

    def own_copy(half, n):
        number = own_number(half)
        ref = packs.at[number] if n == 2 else other.at[half]
        return pltpu.make_async_remote_copy(
            ref.at[half_rows], packs.at[number, half_rows], w_send.at[half, n], w_recv.at[number],
            device_id=(lax.rem(seg + 2 * n, SEGS), me), device_id_type=MESH,
        )

    def send_weights(half):
        facing_copy(own_number(half)).start()
        for n in (1, 3, 2):
            own_copy(half, n).start()

    def facing_copy(number):
        rows = part_rows(plane)
        return pltpu.make_async_remote_copy(
            packs.at[number, rows], packs.at[number, rows], c_send.at[number], c_recv.at[number],
            device_id=(facing, across), device_id_type=MESH,
        )

    def cross_copy(number, plane_of):
        rows = part_rows(plane_of)
        return pltpu.make_async_remote_copy(
            packs.at[number, rows], packs.at[number, rows], x_send.at[number], x_recv.at[number],
            device_id=(seg, across), device_id_type=MESH,
        )

    def sibling_copy(number, start):
        start = pl.multiple_of(start * HALF, 16)
        return pltpu.make_async_remote_copy(
            packs.at[number, pl.ds(start, HALF)],
            packs.at[number, pl.ds(start, HALF)],
            s_send.at[number],
            s_recv.at[number],
            device_id=(seg, sibling),
            device_id_type=MESH,
        )

    def first(number):
        seg_of = source(number)

        @pl.when((seg_of != seg) & (lax.rem(seg_of, 2) == column))
        def _():
            pltpu.make_async_remote_copy(
                packs.at[number, half_rows], packs.at[number, half_rows], w_send.at[0, 0],
                w_recv.at[number], device_id=(facing, across), device_id_type=MESH,
            ).wait_recv()
            facing_copy(number).start()
            sibling_copy(number, core).start()

    def second(number):
        @pl.when(lax.rem(source(number), 2) != column)
        def _():
            rows = part_rows(1 - plane)
            pltpu.make_async_remote_copy(
                packs.at[number, rows], packs.at[number, rows], c_send.at[number],
                c_recv.at[number], device_id=(facing, across), device_id_type=MESH,
            ).wait_recv()
            cross_copy(number, 1 - plane).start()

    def third(number):
        @pl.when(lax.rem(source(number), 2) != column)
        def _():
            cross_copy(number, plane).wait_recv()
            sibling_copy(number, core).start()

    far = max(1, chips // 2)
    pair = min(2, chips)
    at_z = lax.rem(chip, far) * pair + chip // far

    def core_rows(core_of, k):
        start, size = CHUNKS[k]
        return pl.ds(pl.multiple_of(start + core_of * (size // 2), 16), size // 2)

    def plane_rows(plane_of, k):
        start, size = CHUNKS[k]
        start = start + core * (size // 2) + plane_of * (size // 4)
        return pl.ds(pl.multiple_of(start, 16), size // 4)

    def cut_rows(plane_of, k, first_cut, count):
        start, size = CHUNKS[k]
        cut = size // 4 // chips
        start = start + core * (size // 2) + plane_of * (size // 4) + first_cut * cut
        return pl.ds(pl.multiple_of(start, 16), count * cut)

    def pair_rows(plane_of, k):
        return cut_rows(plane_of, k, lax.rem(chip, far) * pair, pair)

    def early_copy(number, rows, send, recv, seg_to, lon_to, ref=None):
        ref = packs.at[number] if ref is None else ref
        return pltpu.make_async_remote_copy(
            ref.at[rows], packs.at[number, rows], send, recv,
            device_id=(seg_to, lon_to), device_id_type=MESH,
        )

    def cut_copy(n, k):
        if n < 4:
            seg_to, lon_to, rows = seg + 2 * n, me, pair_rows(plane, k)
        else:
            seg_to, lon_to, rows = facing + 2 * n, across, pair_rows(1 - plane, k)
        recv = a_recv.at[2 * jnp.minimum(seg, EARLY - 1) + k]
        ref = other.at[0] if n % 2 else packs.at[seg]
        return early_copy(seg, rows, a_send.at[n, k], recv, lax.rem(seg_to, SEGS), lon_to, ref)

    def send_cuts():
        for k in range(2):
            for n in (4, 1, 3, 5, 7, 2, 6):
                cut_copy(n, k).start()

    peers = [n for m in range(1, chips // 2) for n in (m, chips - m)]

    def spread_copy(number, k, n):
        at = 2 * number + k
        rows = cut_rows(plane, k, at_z, 1)
        return early_copy(number, rows, b_send.at[at, n], b_recv.at[at], seg, on_chip(n))

    def spread(number, k):
        @pl.when(seg != number)
        def _():
            at = 2 * number + k
            rows = pair_rows(plane, k)
            early_copy(number, rows, a_send.at[0, 0], a_recv.at[at], seg, across).wait_recv()
            for n in peers:
                spread_copy(number, k, n).start()

    def plane_copy(number, k, plane_of):
        at = 2 * number + k
        rows = plane_rows(plane_of, k)
        return early_copy(number, rows, e_send.at[at], e_recv.at[at], seg, across)

    def cross(number, k):
        @pl.when(seg != number)
        def _():
            if peers:
                at = 2 * number + k
                rows = cut_rows(plane, k, 0, len(peers))
                early_copy(number, rows, a_send.at[0, 0], b_recv.at[at], seg, across).wait_recv()
            plane_copy(number, k, plane).start()

    def core_copy(number, k, core_of):
        at = 2 * number + k
        rows = core_rows(core_of, k)
        return early_copy(number, rows, d_send.at[at], d_recv.at[at], seg, sibling)

    def pair_up(number, k):
        @pl.when(seg != number)
        def _():
            plane_copy(number, k, 1 - plane).wait_recv()
            core_copy(number, k, core).start()

    def halo_copy(number, way):
        return pltpu.make_async_remote_copy(
            hist.at[number, pl.ds(BAND, BAND)],
            hist.at[number, pl.ds(2 * BAND if way == 0 else 0, BAND)],
            h_send.at[number, way],
            h_recv.at[number, way],
            device_id=(seg, west if way == 0 else east),
            device_id_type=MESH,
        )

    swap_copy = pltpu.make_async_remote_copy(
        swap, hist.at[0, pl.ds(BAND, BAND)], swap_sem.at[0], swap_sem.at[1],
        device_id=(seg, place), device_id_type=MESH,
    )

    prepare(0)
    stage[...] = jnp.zeros_like(stage)
    arrival(0, 0).wait()
    micro = order_ref[slot]
    for n in range(6):
        cells = fields_ref[micro, 6 * lat + n].astype(F32)
        for level in range(2):
            start = 72 * level + LON * n
            stage[start : start + LON, :WIDTH] = cells[:, level, :]

    pl.semaphore_wait(barrier, 14 + chips + 3)

    @pl.when(seg < EARLY)
    def _():
        send_cuts()

    @pl.when(seg >= EARLY)
    def _():
        send_weights(0)


    @pl.when(folded)
    def _():
        swap[...] = folded_band(stage[...])
        swap_copy.start()
        swap_copy.wait_recv()

    @pl.when(jnp.logical_not(folded))
    def _():
        hist[0, BAND : 2 * BAND] = folded_band(stage[...])

    for way in range(2):
        halo_copy(0, way).start()
    token = lax.broadcasted_iota(jnp.int32, (TOK, 128), 0)
    token_ref[...] = token.astype(F32)
    share = WIDTH // SEGS
    feature = lax.broadcasted_iota(jnp.int32, (256, 128), 0)
    for g in range(3):
        lane = lanes((256, 128)) - 32 * g
        inside = (lane >= 0) & (lane < share)
        for s in range(SEGS):
            hit = inside & (feature == lane + share * s)
            share_ref[256 * g : 256 * g + 256, 128 * s : 128 * s + 128] = jnp.where(
                hit, 1.0, 0.0
            ).astype(BF)
    lon_ref[...] = lax.rem(token, LON).astype(F32)
    spread(0, 0)
    spread(0, 1)
    cross(0, 0)
    spread(1, 0)
    cross(0, 1)
    spread(1, 1)
    pair_up(0, 0)
    cross(1, 0)
    pair_up(0, 1)
    spread(2, 0)
    prepare(1)
    cross(1, 1)
    spread(2, 1)

    def params(number):
        return packs[number, PARAMS : PARAMS + 16, :].astype(F32)

    def offset(tile):
        row = lax.broadcasted_iota(jnp.int32, (16, 128), 0)
        return jnp.sum(jnp.where(row == 12 + slot, tile, 0.0), axis=0, keepdims=True)

    def step(number, decoder):
        if not decoder:
            @pl.when(number == 0)
            def _():
                @pl.when((seg >= 0) & (seg < 8))
                def _():
                    send_weights(1)

            @pl.when(number == 1)
            def _():
                pair_up(1, 0)
                pair_up(1, 1)
                cross(2, 0)
                cross(2, 1)
                spread(3, 0)
                spread(3, 1)
                first(4)

            @pl.when(number == 2)
            def _():
                pair_up(2, 0)
                pair_up(2, 1)
                cross(3, 0)
                cross(3, 1)
                second(4)
                first(5)

            @pl.when(number == 3)
            def _():
                pair_up(3, 0)
                pair_up(3, 1)
                second(5)
                first(6)
                first(7)

            @pl.when(number == 4)
            def _():
                third(4)
                third(5)
                second(6)

            @pl.when(number == 5)
            def _():
                third(6)
                second(7)

            @pl.when(number == 6)
            def _():
                third(7)

        @pl.when((number >= 7) & (number < SECTIONS - 1))
        def _():
            third(number + 1)

        @pl.when((number >= 6) & (number < SECTIONS - 2))
        def _():
            second(number + 2)

        @pl.when((number >= 4) & (number < SECTIONS - 4))
        def _():
            first(number + 4)

        def early(k):
            for n in range(EARLY):
                @pl.when((number == n) & (seg != n))
                def _():
                    core_copy(n, k, 1 - core).wait_recv()

        @pl.when((source(number) != seg) & (number >= EARLY))
        def _():
            sibling_copy(number, 1 - core).wait_recv()

        if not decoder:
            early(0)

        tile = params(number)
        now = offset(tile)
        if decoder:
            before = offset(params(number - 1))
            earlier = now - offset(params(15 - number))
            aside = taken(pick(token_ref[...], lon_ref[...], earlier), hist, 16 - number)
        else:
            before = offset(params(jnp.maximum(number - 1, 0)))
            before = before * jnp.where(number > 0, 1.0, 0.0)
        chosen = pick(token_ref[...], lon_ref[...], now - before)
        for way in range(2):
            halo_copy(number, way).wait_recv()
        u = taken(chosen, hist, number)
        if decoder:
            u = ((u + aside) * 0.5).astype(BF).astype(F32)
        gain_a = side([tile[0:1] + tile[2:3] + tile[4:5], tile[1:2] + tile[3:4] + tile[5:6]])
        gain_b = side([tile[6:7] + tile[8:9] + tile[10:11], tile[7:8] + tile[9:10] + tile[11:12]])

        def strip(j):
            start = STRIP * j if j < 6 else AFTER + STRIP * (j - 6)
            return packs[number, start : start + STRIP, :]

        def bias(j):
            return packs[number, BIAS + TOK * j : BIAS + TOK * j + TOK, :]

        made = section(
            u, strip, bias, gain_a, gain_b, None if decoder else functools.partial(early, 1)
        )
        hist[number + 1, BAND : 2 * BAND] = folded_band(made)
        for way in range(2):
            halo_copy(number + 1, way).start()

    lax.fori_loop(0, 9, lambda i, c: (step(i, False), c)[1], 0)
    lax.fori_loop(9, SECTIONS, lambda i, c: (step(i, True), c)[1], 0)

    order = lax.broadcasted_iota(jnp.int32, (TOK, 128), 0)
    lon = lax.rem(order, 24) // 2
    token = (lax.rem(order, 2) * 6 + order // 24) * LON + lon
    back = pick(token.astype(F32), lon.astype(F32), -offset(params(SECTIONS - 1)))
    for way in range(2):
        halo_copy(SECTIONS, way).wait_recv()
    final = taken(back, hist, SECTIONS).astype(BF)
    final = side([final[ROWS * g : ROWS * g + ROWS] for g in range(3)])
    final = dot(final, share_ref[...]).astype(BF)
    for s in range(SEGS):
        pieces[s] = final[:, 128 * s : 128 * s + 128]

    def piece_copy(d):
        there = lax.rem(seg + d, SEGS)
        return pltpu.make_async_remote_copy(
            pieces.at[there],
            received.at[seg],
            f_send.at[d],
            f_recv.at[d],
            device_id=(there, place),
            device_id_type=MESH,
        )

    for d in range(1, SEGS):
        piece_copy(d).start()
    mine = pltpu.make_async_copy(pieces.at[seg], received.at[seg], local_sem.at[0])

    @pl.when(folded)
    def _():
        piece_copy(0).start()

    @pl.when(jnp.logical_not(folded))
    def _():
        mine.start()

    def sent(half):
        for n in (1, 2, 3):
            own_copy(half, n).wait_send()

    sent(1)

    @pl.when(seg >= EARLY)
    def _():
        sent(0)

    @pl.when(seg < EARLY)
    def _():
        for k in range(2):
            for n in range(1, SEGS):
                cut_copy(n, k).wait_send()

    def early_sent(number, carry):
        @pl.when(seg != number)
        def _():
            for k in range(2):
                for n in peers:
                    spread_copy(number, k, n).wait_send()
                plane_copy(number, k, plane).wait_send()
                core_copy(number, k, core).wait_send()

        return carry

    def late_sent(number, carry):
        same = lax.rem(source(number), 2) == column

        @pl.when(same)
        def _():
            facing_copy(number).wait_send()

        @pl.when(jnp.logical_not(same))
        def _():
            cross_copy(number, 1 - plane).wait_send()

        return carry

    lax.fori_loop(0, EARLY, early_sent, 0)
    lax.fori_loop(EARLY, SECTIONS, late_sent, 0)

    @pl.when(folded)
    def _():
        swap_copy.wait_send()

    def finish(number, carry):
        @pl.when((number >= EARLY) & (number < SECTIONS) & (source(number) != seg))
        def _():
            sibling_copy(number, core).wait_send()

        for way in range(2):
            halo_copy(number, way).wait_send()
        return carry

    lax.fori_loop(0, SECTIONS + 1, finish, 0)
    for d in range(1, SEGS):
        piece_copy(d).wait()

    @pl.when(folded)
    def _():
        piece_copy(0).wait()

    @pl.when(jnp.logical_not(folded))
    def _():
        mine.wait()

    for m in range(4):
        at = jnp.int32(0)
        for t in range(1, 4):
            at = jnp.where(order_ref[t] == m, 4 * (t // 2) + t % 2, at)
        for a in range(2):
            piece = received[at + 2 * a].astype(F32)
            for g in range(3):
                turned = pltpu.roll(piece, 128 - 32 * g, 1) if g else piece
                out_ref[m, a, ROWS * g : ROWS * g + ROWS] = turned.astype(BF)


def split3(x):
    high = x.astype(BF).astype(F32)
    middle = (x - high).astype(BF).astype(F32)
    return high, middle, x - high - middle


def per_device(
    fields, entry_order, shift_offsets, qkv_weight, out_weight, up_weight, down_weight,
    attn_bias, norm_gain,
):
    dma = pltpu.SemaphoreType.DMA
    stored = (
        fields.transpose(0, 2, 3, 1, 4), qkv_weight[:, 0], out_weight[:, 0], up_weight[:, 0],
        down_weight[:, 0].swapaxes(1, 2), attn_bias[:, 0],
    )
    vmem = pl.BlockSpec(memory_space=pltpu.VMEM)
    smem = pl.BlockSpec(memory_space=pltpu.SMEM)
    got = pl.pallas_call(
        kernel,
        out_shape=jax.ShapeDtypeStruct((4, 2, TOK, 128), BF),
        in_specs=[smem, smem, vmem] + [pl.BlockSpec(memory_space=pl.ANY)] * 6,
        out_specs=vmem,
        scratch_shapes=[pltpu.VMEM(a.shape, a.dtype) for a in stored] + [
            pltpu.VMEM((SECTIONS, PACK, 128), BF),
            pltpu.VMEM((2, PACK, 128), BF),
            pltpu.VMEM((SECTIONS + 1, 3 * BAND, 128), BF),
            pltpu.VMEM((TOK, 128), F32),
            pltpu.VMEM((TOK, 128), F32),
            pltpu.VMEM((768, 1024), BF),
            pltpu.VMEM((TOK, 256), F32),
            pltpu.VMEM((BAND, 128), BF),
            pltpu.VMEM((8, 256), F32),
            pltpu.VMEM((SEGS, ROWS, 128), BF),
            pltpu.VMEM((SEGS, ROWS, 128), BF),
            dma((1,)), dma((2,)), dma((SEGS, 2)), dma((2 * EARLY,)), dma((2 * EARLY, 8)),
            dma((2 * EARLY,)), dma((2 * EARLY,)), dma((2 * EARLY,)), dma((2 * EARLY,)),
            dma((2 * EARLY,)),
            dma((SECTIONS,)), dma((SECTIONS,)), dma((SECTIONS,)), dma((SECTIONS,)), dma((2, 4)),
            dma((SECTIONS,)), dma((SECTIONS,)), dma((SECTIONS,)), dma((SECTIONS + 1, 2)), dma((SECTIONS + 1, 2)), dma((SEGS,)),
            dma((SEGS,)), dma((6, 2)),
        ],
        compiler_params=pltpu.CompilerParams(
            collective_id=0, has_side_effects=True, vmem_limit_bytes=56 * 2**20
        ),
        name="sections",
    )(entry_order, shift_offsets.transpose(1, 2, 0), norm_gain[:, 0], *stored)
    share = WIDTH // SEGS
    got = got[..., :share].reshape(4, 12, LON, 2, share)
    return got.transpose(0, 3, 1, 2, 4)


def solution(mesh):
    placed = (
        P(None, None, None, "lon", None),
        P(),
        P(None, None, "segment"),
        P(None, "segment", None, None),
        P(None, "segment", None, None),
        P(None, "segment", None, None),
        P(None, "segment", None, None),
        P(None, "segment", None, None, None, None),
        P(None, "segment", None, None),
    )
    return jax.shard_map(
        per_device,
        mesh=mesh,
        in_specs=placed,
        out_specs=P(None, None, None, "lon", "segment"),
        check_vma=False,
    )
```

```python
import functools
import math

import jax
import jax.numpy as jnp
from jax import lax
from jax.experimental import pallas as pl
from jax.experimental.pallas import tpu as pltpu
from jax.sharding import PartitionSpec as P

BF = jnp.bfloat16
F32 = jnp.float32
MESH = pl.DeviceIdType.MESH
NT = (((1,), (1,)), ((), ()))
TN = (((0,), (0,)), ((), ()))
NN = (((1,), (0,)), ((), ()))

SEGS = 8
SECTIONS = 16
EARLY = 4
HEADS = 6
TOK = 144
WIDTH = 192
LON = 12
STRIP = 192
BIAS = 6 * STRIP
PARAMS = BIAS + 7 * TOK
AFTER = BIAS + 8 * TOK
PACK = AFTER + 12 * STRIP
HALF = PACK // 2
CHUNKS = ((0, 2560), (2560, 2048))
ROWS = TOK // 3
FOLD = TOK // 2
BAND = TOK + FOLD + 8
EPS = 1e-5
QSCALE = math.log2(math.e) / math.sqrt(32.0)


def dot(a, b, dims=NN):
    return lax.dot_general(a, b, dims, preferred_element_type=F32)


def side(parts):
    return jnp.concatenate(parts, axis=1)


def down(parts):
    return jnp.concatenate(parts, axis=0)


def lanes(shape):
    return lax.broadcasted_iota(jnp.int32, shape, len(shape) - 1)


def normalize(x, gain, inside):
    mean = jnp.sum(x, axis=-1, keepdims=True) * (1.0 / WIDTH)
    centred = x - mean * inside
    spread = jnp.sum(centred * centred, axis=-1, keepdims=True) * (1.0 / WIDTH)
    return (centred * lax.rsqrt(spread + EPS) * gain).astype(BF)


def pick(token, lon, shift):
    x = lon + shift
    west, east = x < 0, x > LON - 1
    block = jnp.where(west, 0.0, jnp.where(east, 2.0, 1.0))
    of = token + shift + jnp.where(west, float(LON), jnp.where(east, float(-LON), 0.0))
    upper = of >= FOLD
    first = block * float(TOK) + of
    second = block * float(BAND - TOK) + jnp.where(upper, of - float(FOLD), of)
    col = lanes((TOK, 128)).astype(F32)

    def hot(hit):
        return jnp.where(hit, 1.0, 0.0).astype(BF)

    take = side([hot(col + float(128 * j) == first) for j in range(4)])[:, : 3 * TOK]
    hits = [col + float(128 * j) == second for j in range(2)]
    rest = down(
        [side([hot(hit & half) for hit in hits]) for half in (jnp.logical_not(upper), upper)]
    )[:, : 3 * (BAND - TOK)]
    return take, rest


def taken(chosen, bands, at):
    take, rest = chosen
    starts = (0, BAND, 2 * BAND)
    first = dot(take, down([bands[at, r : r + TOK, :] for r in starts]))
    second = dot(rest, down([bands[at, r + TOK : r + BAND, :] for r in starts]))
    low = jnp.where(lanes((1, 128)) < 64, 1.0, 0.0)
    second = (second[:TOK] + pltpu.roll(second[TOK:], 64, 1)) * low
    return side([first, second])


def folded_band(h):
    rest = h[:FOLD, 128:] + pltpu.roll(h[FOLD:, 128:], 64, 1)
    return down([h[:, :128], rest, jnp.zeros((8, 128), F32)]).astype(BF)


def section(u, strip, bias, gain_a, gain_b, ready=None):
    col = lanes((1, 256))
    inside = jnp.where(col < WIDTH, 1.0, 0.0)
    low = jnp.where(lanes((1, 128)) < 64, 1.0, 0.0)
    normed = normalize(u, gain_a, inside)
    short = normed[:, :WIDTH]
    qk = dot(short, side([strip(0), strip(1), strip(2)]))
    qb = (qk[:, :256] * QSCALE).astype(BF)
    kb = side([qk[:, 256:], pltpu.roll(qk[:, 128:256], 64, 1)]).astype(BF)
    mixed = strip(4)
    vt = dot(side([strip(3), mixed]), normed, NT).astype(BF)
    zero = jnp.zeros((TOK, 256), BF)
    pos = lanes((TOK, 256))
    spread_q = down(
        [jnp.where((pos >= 32 * h) & (pos < 32 * h + 32), qb, zero) for h in range(HEADS)]
        + [jnp.zeros((32, 256), BF)]
    )
    scores = dot(kb, spread_q, NT) + side([bias(j) for j in range(7)]).astype(F32)
    top = jnp.max(scores, axis=0, keepdims=True)
    expo = jnp.exp2(scores - top)
    inverse = 1.0 / jnp.sum(expo, axis=0, keepdims=True)
    expo = expo.astype(BF)
    parts = []
    for h in range(HEADS):
        cut = slice(128 * h, 128 * h + 256)
        part = dot(vt[32 * h : 32 * h + 32], expo[:, cut]) * inverse[:, cut]
        if h:
            part = pltpu.roll(part, 256 - 16 * h, 1)
        parts.append(part[:, :TOK])
    context = down(parts).astype(BF)
    out = dot(context, side([strip(5), mixed]), TN)
    out = side([out[:, :128], pltpu.roll(out[:, 128:], 64, 1) * low])
    x1 = u + out.astype(BF).astype(F32)
    normed = normalize(x1, gain_b, inside)[:, :WIDTH]
    if ready is not None:
        ready()
    hidden = jax.nn.gelu(dot(normed, side([strip(6 + j) for j in range(6)]))).astype(BF)
    low_t = down([side([strip(12 + j) for j in range(6)]), jnp.zeros((64, 768), BF)])
    y = dot(hidden, low_t, NT)
    return x1 + y


def kernel(
    order_ref, shift_ref, gain_ref, *refs,
):
    given, out_ref, held, rest = refs[:6], refs[6], refs[7:13], refs[13:]
    fields_ref, qkv_ref, out_w_ref, up_ref, low_ref, bias_ref = held
    (
        packs, other, hist, token_ref, lon_ref, share_ref, stage, swap, gains, pieces, received,
        local_sem, swap_sem, a_send, a_recv, b_send, b_recv, e_send, e_recv, d_send,
        d_recv, x_send, x_recv,
        c_send, c_recv, w_send, w_recv, s_send, s_recv, h_send, h_recv, f_send, f_recv,
        in_sem,
    ) = rest
    seg = lax.axis_index("segment")
    me = lax.axis_index("lon")
    ring = lax.axis_size("lon")
    half_ring = ring // 2
    core = lax.rem(me, 2)
    sibling = me + 1 - 2 * core
    column = lax.rem(seg, 2)
    facing = seg + 1 - 2 * column
    slot = column + 2 * (seg // 4)
    lat = lax.rem(seg // 2, 2)
    across = lax.rem(me + half_ring, ring)
    folded = me >= half_ring

    def along(place):
        place = lax.rem(place + ring, ring)
        return jnp.where(place < half_ring, place, 3 * half_ring - 1 - place)

    place = along(me)
    west, east = along(place - 1), along(place + 1)

    def arrival(n, half):
        if n == 0:
            return pltpu.make_async_copy(given[0], held[0], in_sem.at[n, half])
        return pltpu.make_async_copy(given[n].at[half], held[n].at[half], in_sem.at[n, half])

    barrier = pltpu.get_barrier_semaphore()

    def greet(seg_to, lon_to):
        pl.semaphore_signal(barrier, inc=1, device_id=(seg_to, lon_to), device_id_type=MESH)

    for d in (2, 4, 6):
        greet(lax.rem(seg + d, SEGS), me)
    greet(facing, across)
    greet(seg, west)
    greet(seg, east)
    for d in range(1, SEGS):
        greet(lax.rem(seg + d, SEGS), place)
    greet(seg, jnp.where(folded, place, sibling))
    chips = half_ring // 2
    chip = lax.rem(me, half_ring) // 2
    plane = me // half_ring

    def on_chip(n):
        return plane * half_ring + 2 * lax.rem(chip + n, chips) + core

    peers = [n for m in range(1, chips // 2) for n in (m, chips - m)]
    for n in peers:
        greet(seg, on_chip(n))
    greet(seg, across)
    for n in range(1, 4):
        greet(lax.rem(facing + 2 * n, SEGS), across)

    for n in (5, 1, 2, 3, 4, 0):
        arrival(n, 0).start()
    for n in range(1, 6):
        arrival(n, 1).start()

    def source(number):
        return jnp.minimum(number, SECTIONS - 1 - number)

    def own_number(half):
        return seg if half == 0 else SECTIONS - 1 - seg

    def prepare(half):
        number = own_number(half)
        for n in range(1, 6):
            arrival(n, half).wait()

        def put(start, block):
            block = block.astype(BF)
            packs[number, start : start + block.shape[0], :] = block
            other[half, start : start + block.shape[0], :] = block

        def put_strip(j, block):
            put(STRIP * j if j < 6 else AFTER + STRIP * (j - 6), block)

        low = lanes((STRIP, 128)) < 64
        qkv = [qkv_ref[half, :, 128 * j : 128 * j + 128].astype(F32) for j in range(4)]
        put_strip(0, qkv[0])
        put_strip(1, jnp.where(low, qkv[1], qkv[2]))
        put_strip(2, jnp.where(low, pltpu.roll(qkv[1], 64, 1), pltpu.roll(qkv[2], 64, 1)))
        eye = (lax.broadcasted_iota(jnp.int32, (WIDTH, WIDTH), 0) == lanes((WIDTH, WIDTH)))
        turned = dot(jnp.where(eye, 1.0, 0.0).astype(BF), qkv_ref[half, :, 384:576], NT)
        out_w = out_w_ref[half].astype(F32)
        put_strip(3, turned[:, :128])
        put_strip(4, side([turned[:, 128:], out_w[:, 128:]]))
        put_strip(5, out_w[:, :128])
        for j in range(6):
            put_strip(6 + j, up_ref[half, :, 128 * j : 128 * j + 128])
            put_strip(12 + j, low_ref[half, :, 128 * j : 128 * j + 128])

        eye = (lax.broadcasted_iota(jnp.int32, (TOK, TOK), 0) == lanes((TOK, TOK)))
        eye = jnp.where(eye, 1.0, 0.0).astype(BF)

        def put_bias(window, store):
            table = bias_ref[half, window].reshape(HEADS * TOK, TOK)
            top = jnp.max(table, axis=-1, keepdims=True)
            table = ((table - top) * math.log2(math.e)).astype(BF)
            table = dot(eye, down([table, jnp.zeros((32, TOK), BF)]), NT).astype(BF)
            for j in range(7):
                store(BIAS + TOK * j, table[:, 128 * j : 128 * j + 128])

        def store_own(start, block):
            packs[number, start : start + TOK, :] = block

        def store_other(start, block):
            other[half, start : start + TOK, :] = block

        put_bias(lat, store_own)
        put_bias(1 - lat, store_other)
        gains[...] = jnp.zeros_like(gains)
        gains[0:2, :WIDTH] = gain_ref[half]
        rows = []
        for n in range(2):
            for part in split3(gains[n : n + 1, :]):
                rows += [part[:, :128], part[:, 128:]]
        rows += [jnp.full((1, 128), shift_ref[half, 0, t].astype(F32)) for t in range(4)]
        put(PARAMS, down(rows))
        rest = jnp.zeros((TOK - 16, 128), BF)
        put(PARAMS + 16, rest)

    half_rows = pl.ds(pl.multiple_of(core * HALF, 16), HALF)

    def part_rows(plane_of):
        start = core * HALF + plane_of * (HALF // 2)
        return pl.ds(pl.multiple_of(start, 16), HALF // 2)

    def own_copy(half, n):
        number = own_number(half)
        ref = packs.at[number] if n == 2 else other.at[half]
        return pltpu.make_async_remote_copy(
            ref.at[half_rows], packs.at[number, half_rows], w_send.at[half, n], w_recv.at[number],
            device_id=(lax.rem(seg + 2 * n, SEGS), me), device_id_type=MESH,
        )

    def send_weights(half):
        for n in (2, 1, 3):
            own_copy(half, n).start()
        facing_copy(own_number(half)).start()

    def facing_copy(number):
        rows = part_rows(plane)
        return pltpu.make_async_remote_copy(
            packs.at[number, rows], packs.at[number, rows], c_send.at[number], c_recv.at[number],
            device_id=(facing, across), device_id_type=MESH,
        )

    def cross_copy(number, plane_of):
        rows = part_rows(plane_of)
        return pltpu.make_async_remote_copy(
            packs.at[number, rows], packs.at[number, rows], x_send.at[number], x_recv.at[number],
            device_id=(seg, across), device_id_type=MESH,
        )

    def sibling_copy(number, start):
        start = pl.multiple_of(start * HALF, 16)
        return pltpu.make_async_remote_copy(
            packs.at[number, pl.ds(start, HALF)],
            packs.at[number, pl.ds(start, HALF)],
            s_send.at[number],
            s_recv.at[number],
            device_id=(seg, sibling),
            device_id_type=MESH,
        )

    def first(number):
        seg_of = source(number)

        @pl.when((seg_of != seg) & (lax.rem(seg_of, 2) == column))
        def _():
            pltpu.make_async_remote_copy(
                packs.at[number, half_rows], packs.at[number, half_rows], w_send.at[0, 0],
                w_recv.at[number], device_id=(facing, across), device_id_type=MESH,
            ).wait_recv()
            facing_copy(number).start()
            sibling_copy(number, core).start()

    def second(number):
        @pl.when(lax.rem(source(number), 2) != column)
        def _():
            rows = part_rows(1 - plane)
            pltpu.make_async_remote_copy(
                packs.at[number, rows], packs.at[number, rows], c_send.at[number],
                c_recv.at[number], device_id=(facing, across), device_id_type=MESH,
            ).wait_recv()
            cross_copy(number, 1 - plane).start()

    def third(number):
        @pl.when(lax.rem(source(number), 2) != column)
        def _():
            cross_copy(number, plane).wait_recv()
            sibling_copy(number, core).start()

    far = max(1, chips // 2)
    pair = min(2, chips)
    at_z = lax.rem(chip, far) * pair + chip // far

    def core_rows(core_of, k):
        start, size = CHUNKS[k]
        return pl.ds(pl.multiple_of(start + core_of * (size // 2), 16), size // 2)

    def plane_rows(plane_of, k):
        start, size = CHUNKS[k]
        start = start + core * (size // 2) + plane_of * (size // 4)
        return pl.ds(pl.multiple_of(start, 16), size // 4)

    def cut_rows(plane_of, k, first_cut, count):
        start, size = CHUNKS[k]
        cut = size // 4 // chips
        start = start + core * (size // 2) + plane_of * (size // 4) + first_cut * cut
        return pl.ds(pl.multiple_of(start, 16), count * cut)

    def pair_rows(plane_of, k):
        return cut_rows(plane_of, k, lax.rem(chip, far) * pair, pair)

    def early_copy(number, rows, send, recv, seg_to, lon_to, ref=None):
        ref = packs.at[number] if ref is None else ref
        return pltpu.make_async_remote_copy(
            ref.at[rows], packs.at[number, rows], send, recv,
            device_id=(seg_to, lon_to), device_id_type=MESH,
        )

    def cut_copy(n, k):
        if n < 4:
            seg_to, lon_to, rows = seg + 2 * n, me, pair_rows(plane, k)
        else:
            seg_to, lon_to, rows = facing + 2 * n, across, pair_rows(1 - plane, k)
        recv = a_recv.at[2 * jnp.minimum(seg, EARLY - 1) + k]
        ref = other.at[0] if n % 2 else packs.at[seg]
        return early_copy(seg, rows, a_send.at[n, k], recv, lax.rem(seg_to, SEGS), lon_to, ref)

    def send_cuts():
        for k in range(2):
            for n in (4, 1, 3, 5, 7, 2, 6):
                cut_copy(n, k).start()

    def spread_copy(number, k, n):
        at = 2 * number + k
        rows = cut_rows(plane, k, at_z, 1)
        return early_copy(number, rows, b_send.at[at, n], b_recv.at[at], seg, on_chip(n))

    def spread(number, k):
        @pl.when(seg != number)
        def _():
            at = 2 * number + k
            rows = pair_rows(plane, k)
            early_copy(number, rows, a_send.at[0, 0], a_recv.at[at], seg, across).wait_recv()
            for n in peers:
                spread_copy(number, k, n).start()

    def plane_copy(number, k, plane_of):
        at = 2 * number + k
        rows = plane_rows(plane_of, k)
        return early_copy(number, rows, e_send.at[at], e_recv.at[at], seg, across)

    def cross(number, k):
        @pl.when(seg != number)
        def _():
            if peers:
                at = 2 * number + k
                rows = cut_rows(plane, k, 0, len(peers))
                early_copy(number, rows, a_send.at[0, 0], b_recv.at[at], seg, across).wait_recv()
            plane_copy(number, k, plane).start()

    def core_copy(number, k, core_of):
        at = 2 * number + k
        rows = core_rows(core_of, k)
        return early_copy(number, rows, d_send.at[at], d_recv.at[at], seg, sibling)

    def pair_up(number, k):
        @pl.when(seg != number)
        def _():
            plane_copy(number, k, 1 - plane).wait_recv()
            core_copy(number, k, core).start()

    def halo_copy(number, way):
        return pltpu.make_async_remote_copy(
            hist.at[number, pl.ds(BAND, BAND)],
            hist.at[number, pl.ds(2 * BAND if way == 0 else 0, BAND)],
            h_send.at[number, way],
            h_recv.at[number, way],
            device_id=(seg, west if way == 0 else east),
            device_id_type=MESH,
        )

    swap_copy = pltpu.make_async_remote_copy(
        swap, hist.at[0, pl.ds(BAND, BAND)], swap_sem.at[0], swap_sem.at[1],
        device_id=(seg, place), device_id_type=MESH,
    )

    prepare(0)
    stage[...] = jnp.zeros_like(stage)
    arrival(0, 0).wait()
    micro = order_ref[slot]
    for n in range(6):
        cells = fields_ref[micro, 6 * lat + n].astype(F32)
        for level in range(2):
            start = 72 * level + LON * n
            stage[start : start + LON, :WIDTH] = cells[:, level, :]

    pl.semaphore_wait(barrier, 18 + len(peers))

    @pl.when(seg < EARLY)
    def _():
        send_cuts()

    @pl.when(seg >= EARLY)
    def _():
        send_weights(0)


    @pl.when(folded)
    def _():
        swap[...] = folded_band(stage[...])
        swap_copy.start()
        swap_copy.wait_recv()

    @pl.when(jnp.logical_not(folded))
    def _():
        hist[0, BAND : 2 * BAND] = folded_band(stage[...])

    for way in range(2):
        halo_copy(0, way).start()
    token = lax.broadcasted_iota(jnp.int32, (TOK, 128), 0)
    token_ref[...] = token.astype(F32)
    share = WIDTH // SEGS
    feature = lax.broadcasted_iota(jnp.int32, (256, 128), 0)
    for g in range(3):
        lane = lanes((256, 128)) - 32 * g
        inside = (lane >= 0) & (lane < share)
        for s in range(SEGS):
            hit = inside & (feature == lane + share * s)
            share_ref[256 * g : 256 * g + 256, 128 * s : 128 * s + 128] = jnp.where(
                hit, 1.0, 0.0
            ).astype(BF)
    lon_ref[...] = lax.rem(token, LON).astype(F32)
    spread(0, 0)
    spread(0, 1)
    cross(0, 0)
    spread(1, 0)
    cross(0, 1)
    spread(1, 1)
    pair_up(0, 0)
    cross(1, 0)
    pair_up(0, 1)
    spread(2, 0)
    prepare(1)
    cross(1, 1)
    spread(2, 1)

    def params(number):
        return packs[number, PARAMS : PARAMS + 16, :].astype(F32)

    def offset(tile):
        row = lax.broadcasted_iota(jnp.int32, (16, 128), 0)
        return jnp.sum(jnp.where(row == 12 + slot, tile, 0.0), axis=0, keepdims=True)

    def step(number, decoder):
        if not decoder:
            @pl.when(number == 0)
            def _():
                @pl.when((seg >= 0) & (seg < 8))
                def _():
                    send_weights(1)

            @pl.when(number == 1)
            def _():
                pair_up(1, 0)
                pair_up(1, 1)
                cross(2, 0)
                cross(2, 1)
                spread(3, 0)
                spread(3, 1)
                first(4)

            @pl.when(number == 2)
            def _():
                pair_up(2, 0)
                pair_up(2, 1)
                cross(3, 0)
                cross(3, 1)
                second(4)
                first(5)
                first(6)

            @pl.when(number == 3)
            def _():
                pair_up(3, 0)
                pair_up(3, 1)
                second(5)
                first(7)

            @pl.when(number == 4)
            def _():
                third(4)
                third(5)
                second(6)

            @pl.when(number == 5)
            def _():
                third(6)
                second(7)

            @pl.when(number == 6)
            def _():
                third(7)

        @pl.when((number >= 7) & (number < SECTIONS - 1))
        def _():
            third(number + 1)

        @pl.when((number >= 6) & (number < SECTIONS - 2))
        def _():
            second(number + 2)

        @pl.when((number >= 4) & (number < SECTIONS - 4))
        def _():
            first(number + 4)

        def early(k):
            @pl.when((number < EARLY) & (seg != number))
            def _():
                core_copy(number, k, 1 - core).wait_recv()

        @pl.when((source(number) != seg) & (number >= EARLY))
        def _():
            sibling_copy(number, 1 - core).wait_recv()

        if not decoder:
            early(0)

        tile = params(number)
        now = offset(tile)
        if decoder:
            before = offset(params(number - 1))
            earlier = now - offset(params(15 - number))
            aside = taken(pick(token_ref[...], lon_ref[...], earlier), hist, 16 - number)
        else:
            before = offset(params(jnp.maximum(number - 1, 0)))
            before = before * jnp.where(number > 0, 1.0, 0.0)
        chosen = pick(token_ref[...], lon_ref[...], now - before)
        for way in range(2):
            halo_copy(number, way).wait_recv()
        u = taken(chosen, hist, number)
        if decoder:
            u = ((u + aside) * 0.5).astype(BF).astype(F32)
        gain_a = side([tile[0:1] + tile[2:3] + tile[4:5], tile[1:2] + tile[3:4] + tile[5:6]])
        gain_b = side([tile[6:7] + tile[8:9] + tile[10:11], tile[7:8] + tile[9:10] + tile[11:12]])

        def strip(j):
            start = STRIP * j if j < 6 else AFTER + STRIP * (j - 6)
            return packs[number, start : start + STRIP, :]

        def bias(j):
            return packs[number, BIAS + TOK * j : BIAS + TOK * j + TOK, :]

        made = section(
            u, strip, bias, gain_a, gain_b, None if decoder else functools.partial(early, 1)
        )
        hist[number + 1, BAND : 2 * BAND] = folded_band(made)
        for way in range(2):
            halo_copy(number + 1, way).start()

    lax.fori_loop(0, 9, lambda i, c: (step(i, False), c)[1], 0)
    lax.fori_loop(9, SECTIONS, lambda i, c: (step(i, True), c)[1], 0)

    order = lax.broadcasted_iota(jnp.int32, (TOK, 128), 0)
    lon = lax.rem(order, 24) // 2
    token = (lax.rem(order, 2) * 6 + order // 24) * LON + lon
    back = pick(token.astype(F32), lon.astype(F32), -offset(params(SECTIONS - 1)))
    for way in range(2):
        halo_copy(SECTIONS, way).wait_recv()
    final = taken(back, hist, SECTIONS).astype(BF)
    final = side([final[ROWS * g : ROWS * g + ROWS] for g in range(3)])
    final = dot(final, share_ref[...]).astype(BF)
    for s in range(SEGS):
        pieces[s] = final[:, 128 * s : 128 * s + 128]

    def piece_copy(d):
        there = lax.rem(seg + d, SEGS)
        return pltpu.make_async_remote_copy(
            pieces.at[there],
            received.at[seg],
            f_send.at[d],
            f_recv.at[d],
            device_id=(there, place),
            device_id_type=MESH,
        )

    for d in range(1, SEGS):
        piece_copy(d).start()
    mine = pltpu.make_async_copy(pieces.at[seg], received.at[seg], local_sem.at[0])

    @pl.when(folded)
    def _():
        piece_copy(0).start()

    @pl.when(jnp.logical_not(folded))
    def _():
        mine.start()

    def sent(half):
        for n in (1, 2, 3):
            own_copy(half, n).wait_send()

    sent(1)

    @pl.when(seg >= EARLY)
    def _():
        sent(0)

    @pl.when(seg < EARLY)
    def _():
        for k in range(2):
            for n in range(1, SEGS):
                cut_copy(n, k).wait_send()

    def early_sent(number, carry):
        @pl.when(seg != number)
        def _():
            for k in range(2):
                for n in peers:
                    spread_copy(number, k, n).wait_send()
                plane_copy(number, k, plane).wait_send()
                core_copy(number, k, core).wait_send()

        return carry

    def late_sent(number, carry):
        same = lax.rem(source(number), 2) == column

        @pl.when(same)
        def _():
            facing_copy(number).wait_send()

        @pl.when(jnp.logical_not(same))
        def _():
            cross_copy(number, 1 - plane).wait_send()

        return carry

    lax.fori_loop(0, EARLY, early_sent, 0)
    lax.fori_loop(EARLY, SECTIONS, late_sent, 0)

    @pl.when(folded)
    def _():
        swap_copy.wait_send()

    def finish(number, carry):
        @pl.when((number >= EARLY) & (number < SECTIONS) & (source(number) != seg))
        def _():
            sibling_copy(number, core).wait_send()

        for way in range(2):
            halo_copy(number, way).wait_send()
        return carry

    lax.fori_loop(0, SECTIONS + 1, finish, 0)
    for d in range(1, SEGS):
        piece_copy(d).wait()

    @pl.when(folded)
    def _():
        piece_copy(0).wait()

    @pl.when(jnp.logical_not(folded))
    def _():
        mine.wait()

    for m in range(4):
        at = jnp.int32(0)
        for t in range(1, 4):
            at = jnp.where(order_ref[t] == m, 4 * (t // 2) + t % 2, at)
        for a in range(2):
            piece = received[at + 2 * a].astype(F32)
            for g in range(3):
                turned = pltpu.roll(piece, 128 - 32 * g, 1) if g else piece
                out_ref[m, a, ROWS * g : ROWS * g + ROWS] = turned.astype(BF)


def split3(x):
    high = x.astype(BF).astype(F32)
    middle = (x - high).astype(BF).astype(F32)
    return high, middle, x - high - middle


def per_device(
    fields, entry_order, shift_offsets, qkv_weight, out_weight, up_weight, down_weight,
    attn_bias, norm_gain,
):
    dma = pltpu.SemaphoreType.DMA
    stored = (
        fields.transpose(0, 2, 3, 1, 4), qkv_weight[:, 0], out_weight[:, 0], up_weight[:, 0],
        down_weight[:, 0].swapaxes(1, 2), attn_bias[:, 0],
    )
    vmem = pl.BlockSpec(memory_space=pltpu.VMEM)
    smem = pl.BlockSpec(memory_space=pltpu.SMEM)
    got = pl.pallas_call(
        kernel,
        out_shape=jax.ShapeDtypeStruct((4, 2, TOK, 128), BF),
        in_specs=[smem, smem, vmem] + [pl.BlockSpec(memory_space=pl.ANY)] * 6,
        out_specs=vmem,
        scratch_shapes=[pltpu.VMEM(a.shape, a.dtype) for a in stored] + [
            pltpu.VMEM((SECTIONS, PACK, 128), BF),
            pltpu.VMEM((2, PACK, 128), BF),
            pltpu.VMEM((SECTIONS + 1, 3 * BAND, 128), BF),
            pltpu.VMEM((TOK, 128), F32),
            pltpu.VMEM((TOK, 128), F32),
            pltpu.VMEM((768, 1024), BF),
            pltpu.VMEM((TOK, 256), F32),
            pltpu.VMEM((BAND, 128), BF),
            pltpu.VMEM((8, 256), F32),
            pltpu.VMEM((SEGS, ROWS, 128), BF),
            pltpu.VMEM((SEGS, ROWS, 128), BF),
            dma((1,)), dma((2,)), dma((SEGS, 2)), dma((2 * EARLY,)), dma((2 * EARLY, 8)),
            dma((2 * EARLY,)), dma((2 * EARLY,)), dma((2 * EARLY,)), dma((2 * EARLY,)),
            dma((2 * EARLY,)),
            dma((SECTIONS,)), dma((SECTIONS,)), dma((SECTIONS,)), dma((SECTIONS,)), dma((2, 4)),
            dma((SECTIONS,)), dma((SECTIONS,)), dma((SECTIONS,)), dma((SECTIONS + 1, 2)), dma((SECTIONS + 1, 2)), dma((SEGS,)),
            dma((SEGS,)), dma((6, 2)),
        ],
        compiler_params=pltpu.CompilerParams(
            collective_id=0, has_side_effects=True, vmem_limit_bytes=56 * 2**20
        ),
        name="sections",
    )(entry_order, shift_offsets.transpose(1, 2, 0), norm_gain[:, 0], *stored)
    share = WIDTH // SEGS
    got = got[..., :share].reshape(4, 12, LON, 2, share)
    return got.transpose(0, 3, 1, 2, 4)


def solution(mesh):
    placed = (
        P(None, None, None, "lon", None),
        P(),
        P(None, None, "segment"),
        P(None, "segment", None, None),
        P(None, "segment", None, None),
        P(None, "segment", None, None),
        P(None, "segment", None, None),
        P(None, "segment", None, None, None, None),
        P(None, "segment", None, None),
    )
    return jax.shard_map(
        per_device,
        mesh=mesh,
        in_specs=placed,
        out_specs=P(None, None, None, "lon", "segment"),
        check_vma=False,
    )
```
